32 devices in a mesh: dom: 8 (over z, core), feat: 4 (over y, x).
Axes of the slice: x: 2, y: 2, z: 4, core: 2. Of those that a mesh axis runs over, the one named last changes fastest.
Arguments:
- grad_out: bfloat16 [512, 6144], P('feat', 'dom'), may hold values from -6 to 6
- saved_agg: bfloat16 [512, 6144], P('feat', 'dom'), may hold values from -0.1875 to 0.1875
- weight: bfloat16 [512, 512], P('feat'), may hold values from -0.25 to 0.25
- tile_values: bfloat16 [768, 128, 128], P('dom'), may hold values from 0 to 0.029907227
- tile_dst: int32 [768], P('dom'), may hold values from 0 to 5
- tile_slot: int32 [768], P('dom'), may hold values from 0 to 7
- tile_count: int32 [8], P('dom'), may hold values from 12 to 96, as said below
- mirror_owner: int32 [8, 8], P('dom'), may hold values from 0 to 7, each once within a row
- mirror_local: int32 [8, 8], P('dom'), may hold values from 0 to 5
Outputs:
- grad_nodes: bfloat16 [512, 6144], P('feat', 'dom')
- grad_mirrors: bfloat16 [512, 8192], P('feat', 'dom')
- weight_grad: float32 [512, 512], P('feat')
The draws below stay inside these ranges and needn't reach their ends.
Inputs may be any that keep to these rules, and one draw needn't show every extreme that they name: Every partition's first tile_count tiles are live, the rest are padding; some partition has all 96 live in every draw. `mirror_owner`: each partition's row names every partition once.
All inputs are finite; a program needn't handle non-finite values.
Results may differ from the reference program's by a relative error of at most 0.0049.
Values may be sent and summed in bfloat16 or wider, within the bound.
A program may use at most 64 MiB of HBM per device.

```python
import jax
import jax.numpy as jnp
from jax import lax

H = 512
TILE = 128
VB_DEV = 6
TILES_DEV = 96
NODES = 6144
TILES = 768
N_DOM = 8


def draw_tile_count(key, part):
    key = jax.random.fold_in(key, 7)
    first_key, second_key = jax.random.split(key)
    lowest = max(1, TILES_DEV // 8)
    counts = jax.random.randint(first_key, (N_DOM,), lowest, TILES_DEV + 1)
    fullest = jax.random.randint(second_key, (), 0, N_DOM)
    return counts.at[fullest].set(TILES_DEV).astype(jnp.int32)


def touch_ends(array, own_key, least, largest):
    extent = array.shape
    place = [jax.random.randint(jax.random.fold_in(own_key, axis), (), 0, extent[axis]) for axis in range(len(extent))]
    array = array.at[tuple(place)].set(least)
    longest = extent.index(max(extent))
    place[longest] = (place[longest] + 1) % extent[longest]
    return array.at[tuple(place)].set(largest)


def block_levels(stream_key, dims, cuts, smallest, high):
    factor_of = 1.0
    for position, blocks in cuts:
        heights = jax.random.uniform(jax.random.fold_in(jax.random.fold_in(stream_key, 6), position), (blocks,), jnp.float32, smallest / len(cuts), high / len(cuts))
        factor_of = factor_of * jnp.repeat(jnp.exp(heights), dims[position] // blocks).reshape((-1,) + (1,) * (len(dims) - 1 - position))
    return factor_of


def centred(stream_key, shape, width, most, shards=(), held_as=jnp.bfloat16):
    factor_of = block_levels(stream_key, shape, shards, -0.22, 0.18) if shards else 1.0
    values = jax.random.normal(stream_key, shape, jnp.float32) * width * factor_of
    return jnp.minimum(jnp.maximum(values, -most), most).astype(held_as)


def setup_inputs(seed: int = 0) -> dict:
    key_of = jax.random.split(jax.random.key(seed), 10)
    return {
        "grad_out": centred(key_of[0], (H, NODES), 1.0, 6.0, ((0, 4), (1, 8))),
        "saved_agg": centred(key_of[1], (H, NODES), (1.0 / NODES ** 0.5), 0.1875, ((0, 4), (1, 8))),
        "weight": centred(key_of[2], (H, H), H ** -0.5, 0.25, ((0, 4),)),
        "tile_values": jnp.clip(0.029907227 * jax.random.uniform(key_of[3], (TILES, TILE, TILE), jnp.float32) ** block_levels(key_of[3], (TILES, TILE, TILE), ((0, 8),), -0.2, 0.2), 0.0, 0.029907227).astype(jnp.bfloat16),
        "tile_dst": touch_ends(jax.random.randint(key_of[4], (TILES,), 0, VB_DEV), jax.random.fold_in(key_of[4], 1), 0, VB_DEV - 1).astype(jnp.int32),
        "tile_slot": touch_ends(jax.random.randint(key_of[5], (TILES,), 0, N_DOM), jax.random.fold_in(key_of[5], 1), 0, N_DOM - 1).astype(jnp.int32),
        "tile_count": draw_tile_count(jax.random.fold_in(key_of[9], 71), 0),
        "mirror_owner": jax.vmap(lambda own: jax.random.permutation(own, N_DOM))(jax.random.split(key_of[7], N_DOM)).reshape((N_DOM, N_DOM)).astype(jnp.int32),
        "mirror_local": touch_ends(jax.random.randint(key_of[8], (N_DOM, N_DOM), 0, VB_DEV), jax.random.fold_in(key_of[8], 1), 0, VB_DEV - 1).astype(jnp.int32),
    }


def reference(grad_out, saved_agg, weight, tile_values, tile_dst, tile_slot, tile_count, mirror_owner, mirror_local):
    weight_grad = jnp.dot(saved_agg, grad_out.T, preferred_element_type=jnp.float32)
    back_sum = jnp.dot(weight, grad_out, preferred_element_type=jnp.float32).astype(jnp.bfloat16)
    block_total = N_DOM * VB_DEV
    spread = back_sum.reshape(H, block_total, TILE)

    def per_device(carry, device):
        start = device * TILES_DEV
        values = lax.dynamic_slice_in_dim(tile_values, start, TILES_DEV, 0)
        dst_block = lax.dynamic_slice_in_dim(tile_dst, start, TILES_DEV, 0) + device * VB_DEV
        slot_index = lax.dynamic_slice_in_dim(tile_slot, start, TILES_DEV, 0)
        owners = jnp.take(mirror_owner[device], slot_index)
        locals_row = jnp.take(mirror_local[device], slot_index)
        target = (owners * VB_DEV + locals_row).astype(jnp.int32)
        sources = jnp.take(spread, dst_block.astype(jnp.int32), axis=1).astype(jnp.float32)
        products = jnp.einsum("ftk,tkj->tfj", sources, values.astype(jnp.float32))
        live_tiles = (jnp.arange(TILES_DEV, dtype=jnp.int32) < tile_count[device]).astype(jnp.float32)
        products = products * live_tiles[:, None, None]
        return carry.at[target].add(products), None

    start_carry = jnp.zeros((block_total, H, TILE), jnp.float32)
    summed = lax.scan(per_device, start_carry, jnp.arange(N_DOM, dtype=jnp.int32))[0]
    grad_nodes = summed.transpose(1, 0, 2).reshape(H, block_total * TILE).astype(jnp.bfloat16)
    mirror_target = (mirror_owner * VB_DEV + mirror_local).reshape(-1).astype(jnp.int32)
    grad_mirrors = jnp.take(grad_nodes.reshape(H, block_total, TILE), mirror_target, axis=1)
    grad_mirrors = grad_mirrors.reshape(H, N_DOM * N_DOM * TILE)
    return grad_nodes, grad_mirrors, weight_grad
```

```python
import functools

import jax
import jax.numpy as jnp
from jax import lax
from jax.experimental import pallas as pl
from jax.experimental.pallas import tpu as pltpu
from jax.sharding import PartitionSpec as P

MESH = pl.DeviceIdType.MESH
B = 128
F32 = jnp.float32
BF16 = jnp.bfloat16


def kernel(
    n, m, vb, scatter, links, owner, local, g, s, w, tiles,
    gn_out, gm_out, wg_out,
    tbuf, run, adj, allg, spread, meta, mrec, pbuf, prec, msend, gmrec, wpart, wrec, wsum,
    tsem, g_s, g_r, m_s, m_r, p_s, p_r, b_s, b_r, ws_s, ws_r, wg_s, wg_r,
):
    me = lax.axis_index("dom")
    mf = lax.axis_index("feat")
    rows = g.shape[0]
    tile_total = tiles.shape[0]
    chunk = tile_total // 4
    dom_peers = [lax.rem(me + k, n) for k in range(1, n)]
    feat_peers = [lax.rem(mf + k, m) for k in range(1, m)]

    def load_tiles(i):
        return pltpu.make_async_copy(
            tiles.at[pl.ds(i * chunk, chunk)], tbuf.at[pl.ds(i * chunk, chunk)], tsem.at[i]
        )

    for i in range(4):
        load_tiles(i).start()

    barrier = pltpu.get_barrier_semaphore()
    for q in dom_peers:
        pl.semaphore_signal(barrier, inc=1, device_id={"dom": q}, device_id_type=MESH)
    for q in feat_peers:
        pl.semaphore_signal(barrier, inc=1, device_id={"feat": q}, device_id_type=MESH)
    pl.semaphore_wait(barrier, n + m - 2)

    def g_send(q):
        return pltpu.make_async_remote_copy(
            g, allg.at[pl.ds(pl.multiple_of(mf * rows, rows), rows)],
            g_s.at[q], g_r.at[mf], device_id={"feat": q}, device_id_type=MESH,
        )

    def g_recv(q):
        return pltpu.make_async_remote_copy(
            g, allg.at[pl.ds(pl.multiple_of(q * rows, rows), rows)],
            g_s.at[q], g_r.at[q], device_id={"feat": q}, device_id_type=MESH,
        )

    def dom_send(src, dst, send, recv, q):
        return pltpu.make_async_remote_copy(
            src, dst, send.at[q], recv.at[me], device_id={"dom": q}, device_id_type=MESH
        )

    def dom_recv(src, dst, send, recv, q):
        return pltpu.make_async_remote_copy(
            src, dst, send.at[q], recv.at[q], device_id={"dom": q}, device_id_type=MESH
        )

    for q in feat_peers:
        g_send(q).start()
    allg[pl.ds(pl.multiple_of(mf * rows, rows), rows), :] = g[...]

    def slot_of(o):
        return lax.fori_loop(
            0, n, lambda k, acc: jnp.where(owner[0, k] == o, k, acc), jnp.int32(0)
        )

    def fill_meta(o, _):
        value = local[0, slot_of(o)].astype(F32)
        meta[o] = jnp.full((16, B), value, F32).astype(BF16)
        return 0

    lax.fori_loop(0, n, fill_meta, 0)
    for q in dom_peers:
        dom_send(meta.at[q], mrec.at[me], m_s, m_r, q).start()
    mrec[me] = meta[me]

    run[0] = jnp.zeros((B, B), F32)

    def add_tile(t, _):
        run[t + 1] = run[links[t]] + tbuf[t].astype(F32)
        return 0

    for i in range(4):
        load_tiles(i).wait()
        lax.fori_loop(i * chunk, (i + 1) * chunk, add_tile, 0)

    def fill_owner(o, _):
        slot = slot_of(o)
        for d in range(vb):
            adj[d * B : (d + 1) * B, pl.ds(pl.multiple_of(o * B, B), B)] = run[
                links[tile_total + d * n + slot]
            ].astype(BF16)
        return 0

    lax.fori_loop(0, n, fill_owner, 0)

    for q in feat_peers:
        g_recv(q).wait_recv()
    spread[...] = jnp.dot(w[...], allg[...], preferred_element_type=F32).astype(BF16)

    half = n // 2
    mate = me + 1 - 2 * lax.rem(me, 2)
    for i in range(half):
        c = lax.rem(me // 2 + 1 + i, half)
        columns = pl.ds(pl.multiple_of(c * 2 * B, 2 * B), 2 * B)
        part = jnp.dot(spread[...], adj[:, columns], preferred_element_type=F32).astype(BF16)
        pbuf[2 * c] = part[:, :B]
        pbuf[2 * c + 1] = part[:, B:]
        targets = (2 * c, 2 * c + 1) if i < half - 1 else (mate,)
        for q in targets:
            dom_send(pbuf.at[q], prec.at[me], p_s, p_r, q).start()
    prec[me] = pbuf[me]

    wgrad = lax.dot_general(
        s[...], allg[...], (((1,), (1,)), ((), ())), preferred_element_type=F32
    )
    if scatter:
        wrows = rows // n

        def mine(ref, q):
            return ref.at[pl.ds(pl.multiple_of(q * wrows, wrows), wrows)]

        wpart[...] = wgrad.astype(BF16)
        for q in dom_peers:
            dom_send(mine(wpart, q), wrec.at[me], ws_s, ws_r, q).start()
        wrec[me] = wpart[pl.ds(pl.multiple_of(me * wrows, wrows), wrows), :]
    else:
        wg_out[...] = wgrad

    for q in dom_peers:
        dom_recv(meta.at[q], mrec.at[q], m_s, m_r, q).wait_recv()
    for q in dom_peers:
        dom_recv(pbuf.at[q], prec.at[q], p_s, p_r, q).wait_recv()

    rc = 32

    def sum_rows(r, _):
        here = pl.ds(pl.multiple_of(r * rc, rc), rc)
        pick = [mrec[p, 0:1, :].astype(F32) for p in range(n)]
        terms = [prec[p, here, :].astype(F32) for p in range(n)]
        back = [jnp.zeros((rc, B), F32) for _ in range(n)]
        for b in range(vb):
            hot = [jnp.where(pick[p] == b, 1.0, 0.0) for p in range(n)]
            total = terms[0] * hot[0]
            for p in range(1, n):
                total = total + terms[p] * hot[p]
            node = total.astype(BF16)
            gn_out[here, b * B : (b + 1) * B] = node
            node = node.astype(F32)
            back = [back[p] + node * hot[p] for p in range(n)]
        for p in range(n):
            msend[p, here, :] = back[p].astype(BF16)
        return 0

    lax.fori_loop(0, rows // rc, sum_rows, 0)
    for q in dom_peers:
        dom_send(msend.at[q], gmrec.at[me], b_s, b_r, q).start()
    gmrec[me] = msend[me]

    if scatter:
        for q in dom_peers:
            dom_recv(mine(wpart, q), wrec.at[q], ws_s, ws_r, q).wait_recv()
        total = wrec[0].astype(F32)
        for p in range(1, n):
            total = total + wrec[p].astype(F32)
        wsum[...] = total.astype(BF16)
        for q in dom_peers:
            dom_send(wsum, mine(wg_out, me), wg_s, wg_r, q).start()
        wg_out[pl.ds(pl.multiple_of(me * wrows, wrows), wrows), :] = wsum[...]

    for q in dom_peers:
        dom_recv(msend.at[q], gmrec.at[q], b_s, b_r, q).wait_recv()

    def place(slot, _):
        gm_out[:, pl.ds(pl.multiple_of(slot * B, B), B)] = gmrec[owner[0, slot]]
        return 0

    lax.fori_loop(0, n, place, 0)

    if scatter:
        for q in dom_peers:
            dom_recv(wsum, mine(wg_out, q), wg_s, wg_r, q).wait_recv()
    for q in feat_peers:
        g_send(q).wait_send()
    for q in dom_peers:
        dom_send(meta.at[q], mrec.at[me], m_s, m_r, q).wait_send()
        dom_send(pbuf.at[q], prec.at[me], p_s, p_r, q).wait_send()
        dom_send(msend.at[q], gmrec.at[me], b_s, b_r, q).wait_send()
        if scatter:
            dom_send(mine(wpart, q), wrec.at[me], ws_s, ws_r, q).wait_send()
            dom_send(wsum, mine(wg_out, me), wg_s, wg_r, q).wait_send()


def body(
    n, m,
    grad_out, saved_agg, weight, tile_values, tile_dst, tile_slot, tile_count,
    mirror_owner, mirror_local,
):
    rows, vertices = grad_out.shape
    features = weight.shape[1]
    vb = vertices // B
    tile_total = tile_values.shape[0]
    scatter = rows % (16 * n) == 0
    wrows = max(rows // n, 16)

    order = jnp.arange(tile_total, dtype=jnp.int32)
    key = tile_dst * n + tile_slot
    live_key = jnp.where(order < tile_count[0], key, -1)
    query = jnp.concatenate([key, jnp.arange(vb * n, dtype=jnp.int32)])
    limit = jnp.concatenate([order, jnp.full((vb * n,), tile_total, jnp.int32)])
    match = (query[:, None] == live_key[None, :]) & (order[None, :] < limit[:, None])
    links = jnp.max(jnp.where(match, order[None, :] + 1, 0), axis=1)

    vmem = pl.BlockSpec(memory_space=pltpu.VMEM)
    smem = pl.BlockSpec(memory_space=pltpu.SMEM)
    dma = pltpu.SemaphoreType.DMA
    wg_type = BF16 if scatter else F32
    gn, gm, wg = pl.pallas_call(
        functools.partial(kernel, n, m, vb, scatter),
        out_shape=(
            jax.ShapeDtypeStruct((rows, vertices), BF16),
            jax.ShapeDtypeStruct((rows, n * B), BF16),
            jax.ShapeDtypeStruct((rows, features), wg_type),
        ),
        in_specs=[smem] * 3 + [vmem] * 3 + [pl.BlockSpec(memory_space=pl.ANY)],
        out_specs=(vmem, vmem, vmem),
        scratch_shapes=[
            pltpu.VMEM((tile_total, B, B), BF16),
            pltpu.VMEM((tile_total + 1, B, B), F32),
            pltpu.VMEM((vertices, n * B), BF16),
            pltpu.VMEM((features, vertices), BF16),
            pltpu.VMEM((rows, vertices), BF16),
            pltpu.VMEM((n, 16, B), BF16),
            pltpu.VMEM((n, 16, B), BF16),
            pltpu.VMEM((n, rows, B), BF16),
            pltpu.VMEM((n, rows, B), BF16),
            pltpu.VMEM((n, rows, B), BF16),
            pltpu.VMEM((n, rows, B), BF16),
            pltpu.VMEM((rows, features), BF16),
            pltpu.VMEM((n, wrows, features), BF16),
            pltpu.VMEM((wrows, features), BF16),
            dma((4,)),
            dma((m,)), dma((m,)),
            dma((n,)), dma((n,)),
            dma((n,)), dma((n,)),
            dma((n,)), dma((n,)),
            dma((n,)), dma((n,)),
            dma((n,)), dma((n,)),
        ],
        compiler_params=pltpu.CompilerParams(
            collective_id=0, has_side_effects=True, vmem_limit_bytes=48 * 1024 * 1024
        ),
        cost_estimate=pl.CostEstimate(
            flops=2 * rows * vertices * (2 * features + n * B),
            bytes_accessed=2 * tile_total * B * B + 8 * rows * vertices,
            transcendentals=0,
        ),
    )(links, mirror_owner, mirror_local, grad_out, saved_agg, weight, tile_values)
    if scatter:
        wg = wg.astype(F32)
    else:
        wg = lax.psum(wg, "dom")
    return gn, gm, wg


def solution(mesh):
    in_specs = (
        P("feat", "dom"),
        P("feat", "dom"),
        P("feat", None),
        P("dom", None, None),
        P("dom"),
        P("dom"),
        P("dom"),
        P("dom", None),
        P("dom", None),
    )
    out_specs = (P("feat", "dom"), P("feat", "dom"), P("feat", None))
    return jax.shard_map(
        functools.partial(body, mesh.shape["dom"], mesh.shape["feat"]),
        mesh=mesh, in_specs=in_specs, out_specs=out_specs, check_vma=False,
    )
```

```python
import functools

import jax
import jax.numpy as jnp
from jax import lax
from jax.experimental import pallas as pl
from jax.experimental.pallas import tpu as pltpu
from jax.sharding import PartitionSpec as P

MESH = pl.DeviceIdType.MESH
B = 128
F32 = jnp.float32
BF16 = jnp.bfloat16


def kernel(
    n, m, vb, scatter, dst_hbm, slot_hbm, count_hbm, owner_hbm, local_hbm, g, s_hbm, w_hbm, tiles,
    gn_out, gm_out, wg_out,
    dst, slots, count, owner, local, s, w, tbuf, tile_link_v, pair_link_v, tile_link, pair_link,
    slot_of, run, adj, allg, spread, meta, mrec, pbuf, prec, msend, gmrec, gn, gm, wg,
    wpart, wmate, wsend, wrec, wsum,
    lsem, tsem, g_s, g_r, m_s, m_r, p_s, p_r, b_s, b_r, ws_s, ws_r, wg_s, wg_r, x_sem,
):
    me = lax.axis_index("dom")
    mf = lax.axis_index("feat")
    rows = g.shape[0]
    tile_total = tiles.shape[0]
    pairs = vb * n
    chunk = tile_total // 4
    dom_peers = [lax.rem(me + k, n) for k in range(1, n)]
    feat_peers = [lax.rem(mf + k, m) for k in range(1, m)]
    core = lax.rem(me, 2)
    mate = me + 1 - 2 * core
    line_peers = [lax.rem(me + 2 * k, n) for k in range(1, n // 2)]

    def load_tiles(i):
        return pltpu.make_async_copy(
            tiles.at[pl.ds(i * chunk, chunk)], tbuf.at[pl.ds(i * chunk, chunk)], tsem.at[i]
        )

    my_rows = pl.ds(pl.multiple_of(mf * rows, rows), rows)
    loads = [
        pltpu.make_async_copy(a, b, lsem.at[i])
        for i, (a, b) in enumerate(
            [(dst_hbm, dst), (slot_hbm, slots), (count_hbm, count), (owner_hbm, owner),
             (local_hbm, local), (w_hbm, w), (s_hbm, s), (g, allg.at[my_rows])]
        )
    ]
    for load in loads:
        load.start()
    for i in range(4):
        load_tiles(i).start()

    barrier = pltpu.get_barrier_semaphore()
    for q in dom_peers:
        pl.semaphore_signal(barrier, inc=1, device_id={"dom": q}, device_id_type=MESH)
    for q in feat_peers:
        pl.semaphore_signal(barrier, inc=1, device_id={"feat": q}, device_id_type=MESH)
    pl.semaphore_wait(barrier, n + m - 2)

    def g_send(q):
        return pltpu.make_async_remote_copy(
            g, allg.at[pl.ds(pl.multiple_of(mf * rows, rows), rows)],
            g_s.at[q], g_r.at[mf], device_id={"feat": q}, device_id_type=MESH,
        )

    def g_recv(q):
        return pltpu.make_async_remote_copy(
            g, allg.at[pl.ds(pl.multiple_of(q * rows, rows), rows)],
            g_s.at[q], g_r.at[q], device_id={"feat": q}, device_id_type=MESH,
        )

    def dom_send(src, dst, send, recv, q):
        return pltpu.make_async_remote_copy(
            src, dst, send.at[q], recv.at[me], device_id={"dom": q}, device_id_type=MESH
        )

    def dom_recv(src, dst, send, recv, q):
        return pltpu.make_async_remote_copy(
            src, dst, send.at[q], recv.at[q], device_id={"dom": q}, device_id_type=MESH
        )

    for q in feat_peers:
        g_send(q).start()
    for load in loads[:5]:
        load.wait()

    key = dst[...] * n + slots[...]
    across = lax.broadcasted_iota(jnp.int32, (tile_total, tile_total), 1)
    down = lax.broadcasted_iota(jnp.int32, (tile_total, tile_total), 0)
    key_row = jnp.broadcast_to(key, (tile_total, tile_total))
    key_column = jnp.sum(jnp.where(across == down, key_row, 0), axis=1, keepdims=True)
    live_tiles = count[0, 0]
    same = (key_column == key_row) & (down < live_tiles) & (down < across)
    tile_link_v[...] = jnp.max(jnp.where(same, down + 1, 0), axis=0, keepdims=True)
    pair = lax.broadcasted_iota(jnp.int32, (tile_total, pairs), 1)
    down = lax.broadcasted_iota(jnp.int32, (tile_total, pairs), 0)
    same = (key_column == pair) & (down < live_tiles)
    pair_link_v[...] = jnp.max(jnp.where(same, down + 1, 0), axis=0, keepdims=True)
    link_copies = [
        pltpu.make_async_copy(tile_link_v, tile_link, lsem.at[8]),
        pltpu.make_async_copy(pair_link_v, pair_link, lsem.at[9]),
    ]
    for copy in link_copies:
        copy.start()

    def fill_meta(o, _):
        slot = lax.fori_loop(
            0, n, lambda k, acc: jnp.where(owner[0, k] == o, k, acc), jnp.int32(0), unroll=8
        )
        slot_of[o] = slot
        value = local[0, slot].astype(F32)
        meta[o] = jnp.full((16, B), value, F32).astype(BF16)
        return 0

    lax.fori_loop(0, n, fill_meta, 0)
    for q in dom_peers:
        dom_send(meta.at[q], mrec.at[me], m_s, m_r, q).start()
    mrec[me] = meta[me]

    for copy in link_copies:
        copy.wait()
    run[0] = jnp.zeros((B, B), F32)

    def add_tile(t, _):
        run[t + 1] = run[tile_link[0, t]] + tbuf[t].astype(F32)
        return 0

    for i in range(4):
        load_tiles(i).wait()
        lax.fori_loop(i * chunk, (i + 1) * chunk, add_tile, 0, unroll=4)

    def fill_owner(o, _):
        slot = slot_of[o]
        for d in range(vb):
            adj[d * B : (d + 1) * B, pl.ds(pl.multiple_of(o * B, B), B)] = run[
                pair_link[0, d * n + slot]
            ].astype(BF16)
        return 0

    lax.fori_loop(0, n, fill_owner, 0)

    for load in loads[5:]:
        load.wait()
    for q in feat_peers:
        g_recv(q).wait_recv()
    spread[...] = jnp.dot(w[...], allg[...], preferred_element_type=F32).astype(BF16)

    half = n // 2
    for i in range(half):
        c = lax.rem(me // 2 + 1 + i, half)
        columns = pl.ds(pl.multiple_of(c * 2 * B, 2 * B), 2 * B)
        part = jnp.dot(spread[...], adj[:, columns], preferred_element_type=F32).astype(BF16)
        pbuf[2 * c] = part[:, :B]
        pbuf[2 * c + 1] = part[:, B:]
        targets = (2 * c, 2 * c + 1) if i < half - 1 else (mate,)
        for q in targets:
            dom_send(pbuf.at[q], prec.at[me], p_s, p_r, q).start()
    prec[me] = pbuf[me]

    wgrad = lax.dot_general(
        s[...], allg[...], (((1,), (1,)), ((), ())), preferred_element_type=F32
    )
    if scatter:
        wrows = rows // n
        wpart[...] = wgrad.astype(BF16)

        def span(ref, start, size):
            return ref.at[pl.ds(pl.multiple_of(start, wrows), size)]

        def piece(q):
            return (lax.rem(q, 2) * half + q // 2) * wrows

        swap = pltpu.make_async_remote_copy(
            span(wpart, (1 - core) * half * wrows, half * wrows), wmate,
            x_sem.at[0], x_sem.at[1], device_id={"dom": mate}, device_id_type=MESH,
        )
        swap.start()
        swap.wait()
        mine = wpart[pl.ds(pl.multiple_of(core * half * wrows, wrows), half * wrows), :]
        wsend[...] = (mine.astype(F32) + wmate[...].astype(F32)).astype(BF16)
        for q in line_peers:
            dom_send(span(wsend, q // 2 * wrows, wrows), wrec.at[me // 2], ws_s, ws_r, q).start()
        wrec[me // 2] = wsend[pl.ds(pl.multiple_of(me // 2 * wrows, wrows), wrows), :]
    else:
        wg[...] = wgrad
        flush_wg = pltpu.make_async_copy(wg, wg_out, lsem.at[10])
        flush_wg.start()

    for q in dom_peers:
        dom_recv(meta.at[q], mrec.at[q], m_s, m_r, q).wait_recv()
    for q in dom_peers:
        dom_recv(pbuf.at[q], prec.at[q], p_s, p_r, q).wait_recv()

    rc = 32

    def sum_rows(r, _):
        here = pl.ds(pl.multiple_of(r * rc, rc), rc)
        pick = [mrec[p, 0:1, :].astype(F32) for p in range(n)]
        terms = [prec[p, here, :].astype(F32) for p in range(n)]
        back = [jnp.zeros((rc, B), F32) for _ in range(n)]
        for b in range(vb):
            hot = [jnp.where(pick[p] == b, 1.0, 0.0) for p in range(n)]
            total = terms[0] * hot[0]
            for p in range(1, n):
                total = total + terms[p] * hot[p]
            node = total.astype(BF16)
            gn[here, b * B : (b + 1) * B] = node
            node = node.astype(F32)
            back = [back[p] + node * hot[p] for p in range(n)]
        for p in range(n):
            msend[p, here, :] = back[p].astype(BF16)
        return 0

    lax.fori_loop(0, rows // rc, sum_rows, 0)
    for q in dom_peers:
        dom_send(msend.at[q], gmrec.at[me], b_s, b_r, q).start()
    flush_gn = pltpu.make_async_copy(gn, gn_out, lsem.at[11])
    flush_gn.start()
    gmrec[me] = msend[me]

    if scatter:
        for q in line_peers:
            dom_recv(span(wsend, q // 2 * wrows, wrows), wrec.at[q // 2], ws_s, ws_r, q).wait_recv()
        total = wrec[0].astype(F32)
        for p in range(1, half):
            total = total + wrec[p].astype(F32)
        wsum[...] = total.astype(BF16)
        for q in line_peers:
            dom_send(wsum, span(wg, piece(me), wrows), wg_s, wg_r, q).start()
        wg[pl.ds(pl.multiple_of(piece(me), wrows), wrows), :] = wsum[...]
        for q in line_peers:
            dom_recv(wsum, span(wg, piece(q), wrows), wg_s, wg_r, q).wait_recv()
        half_rows = span(wg, core * half * wrows, half * wrows)
        give = pltpu.make_async_remote_copy(
            half_rows, half_rows, x_sem.at[2], x_sem.at[3],
            device_id={"dom": mate}, device_id_type=MESH,
        )
        give.start()

    for q in dom_peers:
        dom_recv(msend.at[q], gmrec.at[q], b_s, b_r, q).wait_recv()

    def place(slot, _):
        gm[:, pl.ds(pl.multiple_of(slot * B, B), B)] = gmrec[owner[0, slot]]
        return 0

    lax.fori_loop(0, n, place, 0, unroll=4)
    flush_gm = pltpu.make_async_copy(gm, gm_out, lsem.at[12])
    flush_gm.start()

    if scatter:
        give.wait()
        flush_wg = pltpu.make_async_copy(wg, wg_out, lsem.at[10])
        flush_wg.start()
    for q in feat_peers:
        g_send(q).wait_send()
    for q in dom_peers:
        dom_send(meta.at[q], mrec.at[me], m_s, m_r, q).wait_send()
        dom_send(pbuf.at[q], prec.at[me], p_s, p_r, q).wait_send()
        dom_send(msend.at[q], gmrec.at[me], b_s, b_r, q).wait_send()
    if scatter:
        for q in line_peers:
            dom_send(span(wsend, q // 2 * wrows, wrows), wrec.at[me // 2], ws_s, ws_r, q).wait_send()
            dom_send(wsum, span(wg, piece(me), wrows), wg_s, wg_r, q).wait_send()
    flush_gn.wait()
    flush_gm.wait()
    flush_wg.wait()


def finish(gn, gm, wg, gn_out, gm_out, wg_out, narrow, wide, sem):
    copies = [
        pltpu.make_async_copy(gn, gn_out, sem.at[0]),
        pltpu.make_async_copy(gm, gm_out, sem.at[1]),
    ]
    load = pltpu.make_async_copy(wg, narrow, sem.at[2])
    load.start()
    for copy in copies:
        copy.start()
    load.wait()
    wide[...] = narrow[...].astype(F32)
    store = pltpu.make_async_copy(wide, wg_out, sem.at[3])
    store.start()
    for copy in copies:
        copy.wait()
    store.wait()


def body(
    n, m,
    grad_out, saved_agg, weight, tile_values, tile_dst, tile_slot, tile_count,
    mirror_owner, mirror_local,
):
    rows, vertices = grad_out.shape
    features = weight.shape[1]
    vb = vertices // B
    tile_total = tile_values.shape[0]
    scatter = rows % (16 * n) == 0
    wrows = max(rows // n, 16)

    hbm = pl.BlockSpec(memory_space=pltpu.HBM)
    int_rows = functools.partial(pltpu.VMEM, dtype=jnp.int32)
    int_smem = functools.partial(pltpu.SMEM, dtype=jnp.int32)
    pairs = vb * n
    dma = pltpu.SemaphoreType.DMA
    wg_type = BF16 if scatter else F32
    gn, gm, wg = pl.pallas_call(
        functools.partial(kernel, n, m, vb, scatter),
        out_shape=(
            jax.ShapeDtypeStruct((rows, vertices), BF16),
            jax.ShapeDtypeStruct((rows, n * B), BF16),
            jax.ShapeDtypeStruct((rows, features), wg_type),
        ),
        in_specs=[hbm] * 9,
        out_specs=(hbm, hbm, hbm),
        scratch_shapes=[
            int_rows((1, tile_total)),
            int_rows((1, tile_total)),
            int_smem((1, 1)),
            int_smem((1, n)),
            int_smem((1, n)),
            pltpu.VMEM((rows, vertices), BF16),
            pltpu.VMEM((rows, features), BF16),
            pltpu.VMEM((tile_total, B, B), BF16),
            int_rows((1, tile_total)),
            int_rows((1, pairs)),
            int_smem((1, tile_total)),
            int_smem((1, pairs)),
            int_smem((n,)),
            pltpu.VMEM((tile_total + 1, B, B), F32),
            pltpu.VMEM((vertices, n * B), BF16),
            pltpu.VMEM((features, vertices), BF16),
            pltpu.VMEM((rows, vertices), BF16),
            pltpu.VMEM((n, 16, B), BF16),
            pltpu.VMEM((n, 16, B), BF16),
            pltpu.VMEM((n, rows, B), BF16),
            pltpu.VMEM((n, rows, B), BF16),
            pltpu.VMEM((n, rows, B), BF16),
            pltpu.VMEM((n, rows, B), BF16),
            pltpu.VMEM((rows, vertices), BF16),
            pltpu.VMEM((rows, n * B), BF16),
            pltpu.VMEM((rows, features), wg_type),
            pltpu.VMEM((rows, features), BF16),
            pltpu.VMEM((wrows * n // 2, features), BF16),
            pltpu.VMEM((wrows * n // 2, features), BF16),
            pltpu.VMEM((n // 2, wrows, features), BF16),
            pltpu.VMEM((wrows, features), BF16),
            dma((13,)),
            dma((4,)),
            dma((m,)), dma((m,)),
            dma((n,)), dma((n,)),
            dma((n,)), dma((n,)),
            dma((n,)), dma((n,)),
            dma((n,)), dma((n,)),
            dma((n,)), dma((n,)),
            dma((4,)),
        ],
        compiler_params=pltpu.CompilerParams(
            collective_id=0, has_side_effects=True, vmem_limit_bytes=62 * 1024 * 1024
        ),
        cost_estimate=pl.CostEstimate(
            flops=2 * rows * vertices * (2 * features + n * B),
            bytes_accessed=2 * tile_total * B * B + 8 * rows * vertices,
            transcendentals=0,
        ),
    )(
        tile_dst.reshape(1, -1), tile_slot.reshape(1, -1), tile_count.reshape(1, 1),
        mirror_owner, mirror_local, grad_out, saved_agg, weight, tile_values,
    )
    if scatter:
        return pl.pallas_call(
            finish,
            out_shape=(
                jax.ShapeDtypeStruct(gn.shape, BF16),
                jax.ShapeDtypeStruct(gm.shape, BF16),
                jax.ShapeDtypeStruct(wg.shape, F32),
            ),
            in_specs=[hbm] * 3,
            out_specs=(hbm, hbm, hbm),
            scratch_shapes=[
                pltpu.VMEM(wg.shape, BF16), pltpu.VMEM(wg.shape, F32), dma((4,))
            ],
        )(gn, gm, wg)
    else:
        wg = lax.psum(wg, "dom")
    return gn, gm, wg


def solution(mesh):
    in_specs = (
        P("feat", "dom"),
        P("feat", "dom"),
        P("feat", None),
        P("dom", None, None),
        P("dom"),
        P("dom"),
        P("dom"),
        P("dom", None),
        P("dom", None),
    )
    out_specs = (P("feat", "dom"), P("feat", "dom"), P("feat", None))
    return jax.shard_map(
        functools.partial(body, mesh.shape["dom"], mesh.shape["feat"]),
        mesh=mesh, in_specs=in_specs, out_specs=out_specs, check_vma=False,
    )
```

```python
import functools

import jax
import jax.numpy as jnp
from jax import lax
from jax.experimental import pallas as pl
from jax.experimental.pallas import tpu as pltpu
from jax.sharding import PartitionSpec as P

MESH = pl.DeviceIdType.MESH
B = 128
F32 = jnp.float32
BF16 = jnp.bfloat16


def kernel(
    n, m, vb, scatter, dst_hbm, slot_hbm, count_hbm, owner_hbm, local_hbm, g, s_hbm, w_hbm, tiles,
    gn_out, gm_out, wg_out,
    dst, slots, count, owner, local, s, w, tbuf, tile_link_v, pair_link_v, tile_link, pair_link,
    slot_of, run, adj, allg, spread, meta, mrec, pbuf, prec, msend, gmrec0, gmrec1, gn, gm, wg,
    wpart, wmate, wsend, wrec, wsum,
    lsem, tsem, g_s, g_r, m_s, m_r, p_s, p_r, b_s, b_r, ws_s, ws_r, wg_s, wg_r, x_sem,
):
    me = lax.axis_index("dom")
    mf = lax.axis_index("feat")
    rows = g.shape[0]
    tile_total = tiles.shape[0]
    pairs = vb * n
    chunk = tile_total // 4
    dom_peers = [lax.rem(me + k, n) for k in range(1, n)]
    feat_peers = [lax.rem(mf + k, m) for k in range(1, m)]
    core = lax.rem(me, 2)
    mate = me + 1 - 2 * core
    line_peers = [lax.rem(me + 2 * k, n) for k in range(1, n // 2)]

    def load_tiles(i):
        return pltpu.make_async_copy(
            tiles.at[pl.ds(i * chunk, chunk)], tbuf.at[pl.ds(i * chunk, chunk)], tsem.at[i]
        )

    my_rows = pl.ds(pl.multiple_of(mf * rows, rows), rows)
    loads = [
        pltpu.make_async_copy(a, b, lsem.at[i])
        for i, (a, b) in enumerate(
            [(dst_hbm, dst), (slot_hbm, slots), (count_hbm, count), (owner_hbm, owner),
             (local_hbm, local), (w_hbm, w), (s_hbm, s), (g, allg.at[my_rows])]
        )
    ]
    for load in loads:
        load.start()
    for i in range(4):
        load_tiles(i).start()

    barrier = pltpu.get_barrier_semaphore()
    for q in dom_peers:
        pl.semaphore_signal(barrier, inc=1, device_id={"dom": q}, device_id_type=MESH)
    for q in feat_peers:
        pl.semaphore_signal(barrier, inc=1, device_id={"feat": q}, device_id_type=MESH)
    pl.semaphore_wait(barrier, n + m - 2)

    half_rows = rows // 2
    square = m == 4
    near = mf + 1 - 2 * lax.rem(mf, 2)
    far = lax.rem(mf + 2, 4)
    across_both = lax.rem(near + 2, 4)

    def g_copy(source, part, sem, to, whole=False):
        size = rows if whole else half_rows
        start = source * rows + part * half_rows
        there = allg.at[pl.ds(pl.multiple_of(start, half_rows), size)]
        here = there
        if source is mf:
            here = g.at[pl.ds(part * half_rows, size)]
        return pltpu.make_async_remote_copy(
            here, there, g_s.at[sem], g_r.at[sem], device_id={"feat": to}, device_id_type=MESH
        )

    if square:
        own_sends = [
            g_copy(mf, 0, 0, near), g_copy(mf, 1, 2, far),
            g_copy(mf, 1, 1, near), g_copy(mf, 0, 3, far),
        ]
        passed = [g_copy(near, 0, 4, far), g_copy(far, 1, 5, near)]
        first = [g_copy(near, 0, 0, near), g_copy(far, 1, 2, far)]
        second = [g_copy(near, 1, 1, near), g_copy(far, 0, 3, far)]
        last = [g_copy(across_both, 0, 4, far), g_copy(across_both, 1, 5, near)]
    else:
        own_sends = [g_copy(mf, 0, k, q, True) for k, q in enumerate(feat_peers)]
        passed, first, second = [], [], []
        last = [
            g_copy(lax.rem(mf + m - 1 - k, m), 0, k, mf, True) for k in range(m - 1)
        ]

    def dom_send(src, dst, send, recv, q):
        return pltpu.make_async_remote_copy(
            src, dst, send.at[q], recv.at[me], device_id={"dom": q}, device_id_type=MESH
        )

    def dom_recv(src, dst, send, recv, q):
        return pltpu.make_async_remote_copy(
            src, dst, send.at[q], recv.at[q], device_id={"dom": q}, device_id_type=MESH
        )

    for copy in own_sends:
        copy.start()
    for load in loads[:5]:
        load.wait()

    key = dst[...] * n + slots[...]
    across = lax.broadcasted_iota(jnp.int32, (tile_total, tile_total), 1)
    down = lax.broadcasted_iota(jnp.int32, (tile_total, tile_total), 0)
    key_row = jnp.broadcast_to(key, (tile_total, tile_total))
    key_column = jnp.sum(jnp.where(across == down, key_row, 0), axis=1, keepdims=True)
    live_tiles = count[0, 0]
    same = (key_column == key_row) & (down < live_tiles) & (down < across)
    tile_link_v[...] = jnp.max(jnp.where(same, down + 1, 0), axis=0, keepdims=True)
    pair = lax.broadcasted_iota(jnp.int32, (tile_total, pairs), 1)
    down = lax.broadcasted_iota(jnp.int32, (tile_total, pairs), 0)
    same = (key_column == pair) & (down < live_tiles)
    pair_link_v[...] = jnp.max(jnp.where(same, down + 1, 0), axis=0, keepdims=True)
    link_copies = [
        pltpu.make_async_copy(tile_link_v, tile_link, lsem.at[8]),
        pltpu.make_async_copy(pair_link_v, pair_link, lsem.at[9]),
    ]
    for copy in link_copies:
        copy.start()

    def fill_meta(o, _):
        slot = lax.fori_loop(
            0, n, lambda k, acc: jnp.where(owner[0, k] == o, k, acc), jnp.int32(0), unroll=8
        )
        slot_of[o] = slot
        value = local[0, slot].astype(F32)
        meta[o] = jnp.full((16, B), value, F32).astype(BF16)
        return 0

    lax.fori_loop(0, n, fill_meta, 0)
    for q in dom_peers:
        dom_send(meta.at[q], mrec.at[me], m_s, m_r, q).start()
    mrec[me] = meta[me]

    for copy in link_copies:
        copy.wait()
    run[0] = jnp.zeros((B, B), F32)

    def add_tile(t, _):
        run[t + 1] = run[tile_link[0, t]] + tbuf[t].astype(F32)
        return 0

    for i in range(4):
        load_tiles(i).wait()
        lax.fori_loop(i * chunk, (i + 1) * chunk, add_tile, 0, unroll=4)
        if i == 1:
            for arrived, on in zip(first, passed):
                arrived.wait_recv()
                on.start()

    def fill_owner(o, _):
        slot = slot_of[o]
        for d in range(vb):
            adj[d * B : (d + 1) * B, pl.ds(pl.multiple_of(o * B, B), B)] = run[
                pair_link[0, d * n + slot]
            ].astype(BF16)
        return 0

    lax.fori_loop(0, n, fill_owner, 0)

    for load in loads[5:]:
        load.wait()
    for copy in second + last:
        copy.wait_recv()
    spread[...] = jnp.dot(w[...], allg[...], preferred_element_type=F32).astype(BF16)

    half = n // 2
    def p_copy(h, q, sending):
        recv = p_r.at[h * n + (me if sending else q)]
        return pltpu.make_async_remote_copy(
            pbuf.at[h, q], prec.at[h, me if sending else q], p_s.at[h * n + q], recv,
            device_id={"dom": q}, device_id_type=MESH,
        )

    gmrec = (gmrec0, gmrec1)

    def b_copy(h, q, sending):
        recv = b_r.at[h * n + (me if sending else q)]
        return pltpu.make_async_remote_copy(
            msend.at[h, q], gmrec[h].at[me if sending else q], b_s.at[h * n + q], recv,
            device_id={"dom": q}, device_id_type=MESH,
        )

    order = []
    for i in range(half):
        c = lax.rem(me // 2 + 1 + i, half)
        columns = pl.ds(pl.multiple_of(c * 2 * B, 2 * B), 2 * B)
        part = jnp.dot(spread[...], adj[:, columns], preferred_element_type=F32).astype(BF16)
        for h in range(2):
            pbuf[h, 2 * c] = part[h * half_rows : (h + 1) * half_rows, :B]
            pbuf[h, 2 * c + 1] = part[h * half_rows : (h + 1) * half_rows, B:]
        targets = (2 * c, 2 * c + 1) if i < half - 1 else (mate,)
        for q in targets:
            p_copy(0, q, True).start()
            order.append(q)
    for q in order:
        p_copy(1, q, True).start()
    for h in range(2):
        prec[h, me] = pbuf[h, me]

    wgrad = lax.dot_general(
        s[...], allg[...], (((1,), (1,)), ((), ())), preferred_element_type=F32
    )
    if scatter:
        wrows = rows // n
        wpart[...] = wgrad.astype(BF16)

        def span(ref, start, size):
            return ref.at[pl.ds(pl.multiple_of(start, wrows), size)]

        def piece(q):
            return (lax.rem(q, 2) * half + q // 2) * wrows

        swap = pltpu.make_async_remote_copy(
            span(wpart, (1 - core) * half * wrows, half * wrows), wmate,
            x_sem.at[0], x_sem.at[1], device_id={"dom": mate}, device_id_type=MESH,
        )
        swap.start()
    else:
        wg[...] = wgrad
        flush_wg = pltpu.make_async_copy(wg, wg_out, lsem.at[10])
        flush_wg.start()

    for q in dom_peers:
        dom_recv(meta.at[q], mrec.at[q], m_s, m_r, q).wait_recv()
    rc = min(32, half_rows)

    def sum_rows(h, r, _):
        here = pl.ds(pl.multiple_of(r * rc, rc), rc)
        there = pl.ds(pl.multiple_of(h * half_rows + r * rc, rc), rc)
        pick = [mrec[p, 0:1, :].astype(F32) for p in range(n)]
        terms = [prec[h, p, here, :].astype(F32) for p in range(n)]
        back = [jnp.zeros((rc, B), F32) for _ in range(n)]
        for b in range(vb):
            hot = [jnp.where(pick[p] == b, 1.0, 0.0) for p in range(n)]
            total = terms[0] * hot[0]
            for p in range(1, n):
                total = total + terms[p] * hot[p]
            node = total.astype(BF16)
            gn[there, b * B : (b + 1) * B] = node
            node = node.astype(F32)
            back = [back[p] + node * hot[p] for p in range(n)]
        for p in range(n):
            msend[h, p, here, :] = back[p].astype(BF16)
        return 0

    for h in range(2):
        for q in order:
            p_copy(h, q, False).wait_recv()
        lax.fori_loop(0, half_rows // rc, functools.partial(sum_rows, h), 0)
        for q in order:
            b_copy(h, q, True).start()
        gmrec[h][me] = msend[h, me]
        if scatter and h == 0:
            swap.wait()
            mine = wpart[pl.ds(pl.multiple_of(core * half * wrows, wrows), half * wrows), :]
            wsend[...] = (mine.astype(F32) + wmate[...].astype(F32)).astype(BF16)
            for q in line_peers:
                dom_send(span(wsend, q // 2 * wrows, wrows), wrec.at[me // 2], ws_s, ws_r, q).start()
            wrec[me // 2] = wsend[pl.ds(pl.multiple_of(me // 2 * wrows, wrows), wrows), :]
    flush_gn = pltpu.make_async_copy(gn, gn_out, lsem.at[11])
    flush_gn.start()
    if scatter:
        for q in line_peers:
            dom_recv(span(wsend, q // 2 * wrows, wrows), wrec.at[q // 2], ws_s, ws_r, q).wait_recv()
        total = wrec[0].astype(F32)
        for p in range(1, half):
            total = total + wrec[p].astype(F32)
        wsum[...] = total.astype(BF16)
        for q in line_peers:
            dom_send(wsum, span(wg, piece(me), wrows), wg_s, wg_r, q).start()
        wg[pl.ds(pl.multiple_of(piece(me), wrows), wrows), :] = wsum[...]
        for q in line_peers:
            dom_recv(wsum, span(wg, piece(q), wrows), wg_s, wg_r, q).wait_recv()
        kept = span(wg, core * half * wrows, half * wrows)
        give = pltpu.make_async_remote_copy(
            kept, kept, x_sem.at[2], x_sem.at[3],
            device_id={"dom": mate}, device_id_type=MESH,
        )
        give.start()

    def place(h, slot, _):
        gm[h * half_rows : (h + 1) * half_rows, pl.ds(pl.multiple_of(slot * B, B), B)] = gmrec[h][
            owner[0, slot]
        ]
        return 0

    flush_gm = []
    for h in range(2):
        for q in order:
            b_copy(h, q, False).wait_recv()
        lax.fori_loop(0, n, functools.partial(place, h), 0, unroll=4)
        part = pl.ds(h * half_rows, half_rows)
        flush_gm.append(pltpu.make_async_copy(gm.at[part], gm_out.at[part], lsem.at[12 + h]))
        flush_gm[h].start()

    if scatter:
        give.wait()
        flush_wg = pltpu.make_async_copy(wg, wg_out, lsem.at[10])
        flush_wg.start()
    for copy in own_sends + passed:
        copy.wait_send()
    for q in dom_peers:
        dom_send(meta.at[q], mrec.at[me], m_s, m_r, q).wait_send()
        for h in range(2):
            p_copy(h, q, True).wait_send()
            b_copy(h, q, True).wait_send()
    if scatter:
        for q in line_peers:
            dom_send(span(wsend, q // 2 * wrows, wrows), wrec.at[me // 2], ws_s, ws_r, q).wait_send()
            dom_send(wsum, span(wg, piece(me), wrows), wg_s, wg_r, q).wait_send()
    flush_gn.wait()
    for copy in flush_gm:
        copy.wait()
    flush_wg.wait()


def finish(gn, gm, wg, gn_out, gm_out, wg_out, gn_v, gm_v, narrow, wide, sem):
    pairs = ((wg, narrow, wide, wg_out), (gm, gm_v, gm_v, gm_out), (gn, gn_v, gn_v, gn_out))
    loads = [pltpu.make_async_copy(p[0], p[1], sem.at[k]) for k, p in enumerate(pairs)]
    stores = [pltpu.make_async_copy(p[2], p[3], sem.at[3 + k]) for k, p in enumerate(pairs)]
    for load in loads:
        load.start()
    loads[0].wait()
    wide[...] = narrow[...].astype(F32)
    stores[0].start()
    for k in (1, 2):
        loads[k].wait()
        stores[k].start()
    for store in stores:
        store.wait()


def body(
    n, m,
    grad_out, saved_agg, weight, tile_values, tile_dst, tile_slot, tile_count,
    mirror_owner, mirror_local,
):
    rows, vertices = grad_out.shape
    features = weight.shape[1]
    vb = vertices // B
    tile_total = tile_values.shape[0]
    scatter = rows % (16 * n) == 0
    wrows = max(rows // n, 16)

    hbm = pl.BlockSpec(memory_space=pltpu.HBM)
    int_rows = functools.partial(pltpu.VMEM, dtype=jnp.int32)
    int_smem = functools.partial(pltpu.SMEM, dtype=jnp.int32)
    pairs = vb * n
    dma = pltpu.SemaphoreType.DMA
    wg_type = BF16 if scatter else F32
    gn, gm, wg = pl.pallas_call(
        functools.partial(kernel, n, m, vb, scatter),
        out_shape=(
            jax.ShapeDtypeStruct((rows, vertices), BF16),
            jax.ShapeDtypeStruct((rows, n * B), BF16),
            jax.ShapeDtypeStruct((rows, features), wg_type),
        ),
        in_specs=[hbm] * 9,
        out_specs=(hbm, hbm, hbm),
        scratch_shapes=[
            int_rows((1, tile_total)),
            int_rows((1, tile_total)),
            int_smem((1, 1)),
            int_smem((1, n)),
            int_smem((1, n)),
            pltpu.VMEM((rows, vertices), BF16),
            pltpu.VMEM((rows, features), BF16),
            pltpu.VMEM((tile_total, B, B), BF16),
            int_rows((1, tile_total)),
            int_rows((1, pairs)),
            int_smem((1, tile_total)),
            int_smem((1, pairs)),
            int_smem((n,)),
            pltpu.VMEM((tile_total + 1, B, B), F32),
            pltpu.VMEM((vertices, n * B), BF16),
            pltpu.VMEM((features, vertices), BF16),
            pltpu.VMEM((rows, vertices), BF16),
            pltpu.VMEM((n, 16, B), BF16),
            pltpu.VMEM((n, 16, B), BF16),
            pltpu.VMEM((2, n, rows // 2, B), BF16),
            pltpu.VMEM((2, n, rows // 2, B), BF16),
            pltpu.VMEM((2, n, rows // 2, B), BF16),
            pltpu.VMEM((n, rows // 2, B), BF16),
            pltpu.VMEM((n, rows // 2, B), BF16),
            pltpu.VMEM((rows, vertices), BF16),
            pltpu.VMEM((rows, n * B), BF16),
            pltpu.VMEM((rows, features), wg_type),
            pltpu.VMEM((rows, features), BF16),
            pltpu.VMEM((wrows * n // 2, features), BF16),
            pltpu.VMEM((wrows * n // 2, features), BF16),
            pltpu.VMEM((n // 2, wrows, features), BF16),
            pltpu.VMEM((wrows, features), BF16),
            dma((14,)),
            dma((4,)),
            dma((max(m, 6),)), dma((max(m, 6),)),
            dma((n,)), dma((n,)),
            dma((2 * n,)), dma((2 * n,)),
            dma((2 * n,)), dma((2 * n,)),
            dma((n,)), dma((n,)),
            dma((n,)), dma((n,)),
            dma((4,)),
        ],
        compiler_params=pltpu.CompilerParams(
            collective_id=0, has_side_effects=True, vmem_limit_bytes=62 * 1024 * 1024
        ),
        cost_estimate=pl.CostEstimate(
            flops=2 * rows * vertices * (2 * features + n * B),
            bytes_accessed=2 * tile_total * B * B + 8 * rows * vertices,
            transcendentals=0,
        ),
    )(
        tile_dst.reshape(1, -1), tile_slot.reshape(1, -1), tile_count.reshape(1, 1),
        mirror_owner, mirror_local, grad_out, saved_agg, weight, tile_values,
    )
    if scatter:
        return pl.pallas_call(
            finish,
            out_shape=(
                jax.ShapeDtypeStruct(gn.shape, BF16),
                jax.ShapeDtypeStruct(gm.shape, BF16),
                jax.ShapeDtypeStruct(wg.shape, F32),
            ),
            in_specs=[hbm] * 3,
            out_specs=(hbm, hbm, hbm),
            scratch_shapes=[
                pltpu.VMEM(gn.shape, BF16), pltpu.VMEM(gm.shape, BF16),
                pltpu.VMEM(wg.shape, BF16), pltpu.VMEM(wg.shape, F32), dma((6,)),
            ],
        )(gn, gm, wg)
    else:
        wg = lax.psum(wg, "dom")
    return gn, gm, wg


def solution(mesh):
    in_specs = (
        P("feat", "dom"),
        P("feat", "dom"),
        P("feat", None),
        P("dom", None, None),
        P("dom"),
        P("dom"),
        P("dom"),
        P("dom", None),
        P("dom", None),
    )
    out_specs = (P("feat", "dom"), P("feat", "dom"), P("feat", None))
    return jax.shard_map(
        functools.partial(body, mesh.shape["dom"], mesh.shape["feat"]),
        mesh=mesh, in_specs=in_specs, out_specs=out_specs, check_vma=False,
    )
```

```python
import functools

import jax
import jax.numpy as jnp
from jax import lax
from jax.experimental import pallas as pl
from jax.experimental.pallas import tpu as pltpu
from jax.sharding import PartitionSpec as P

MESH = pl.DeviceIdType.MESH
B = 128
F32 = jnp.float32
BF16 = jnp.bfloat16


def kernel(
    n, m, vb, scatter, dst_hbm, slot_hbm, count_hbm, owner_hbm, local_hbm, g, s_hbm, w_hbm, tiles,
    gn_out, gm_out, wg_out,
    dst, slots, count, owner, local, s, w, tbuf, tile_order_v, joins_v, pair_end_v, tile_order,
    joins, pair_end,
    slot_of, run, adj, allg, spread, meta, mrec, pbuf, prec, msend, gmrec0, gmrec1, gn, gm, wg,
    wpart, wmate, wsend, wrec, wsum,
    lsem, tsem, g_s, g_r, m_s, m_r, p_s, p_r, b_s, b_r, ws_s, ws_r, wg_s, wg_r, x_sem,
):
    me = lax.axis_index("dom")
    mf = lax.axis_index("feat")
    rows = g.shape[0]
    tile_total = tiles.shape[0]
    pairs = vb * n
    chunk = tile_total // 4
    dom_peers = [lax.rem(me + k, n) for k in range(1, n)]
    feat_peers = [lax.rem(mf + k, m) for k in range(1, m)]
    core = lax.rem(me, 2)
    mate = me + 1 - 2 * core
    line_peers = [lax.rem(me + 2 * k, n) for k in range(1, n // 2)]

    def load_tiles(i):
        return pltpu.make_async_copy(
            tiles.at[pl.ds(i * chunk, chunk)], tbuf.at[pl.ds(i * chunk, chunk)], tsem.at[i]
        )

    my_rows = pl.ds(pl.multiple_of(mf * rows, rows), rows)
    loads = [
        pltpu.make_async_copy(a, b, lsem.at[i])
        for i, (a, b) in enumerate(
            [(dst_hbm, dst), (slot_hbm, slots), (count_hbm, count), (owner_hbm, owner),
             (local_hbm, local), (w_hbm, w), (s_hbm, s), (g, allg.at[my_rows])]
        )
    ]
    for load in loads:
        load.start()
    for i in range(4):
        load_tiles(i).start()

    barrier = pltpu.get_barrier_semaphore()
    for q in dom_peers:
        pl.semaphore_signal(barrier, inc=1, device_id={"dom": q}, device_id_type=MESH)
    for q in feat_peers:
        pl.semaphore_signal(barrier, inc=1, device_id={"feat": q}, device_id_type=MESH)
    pl.semaphore_wait(barrier, n + m - 2)

    half_rows = rows // 2
    square = m == 4
    near = mf + 1 - 2 * lax.rem(mf, 2)
    far = lax.rem(mf + 2, 4)
    across_both = lax.rem(near + 2, 4)

    def g_copy(source, part, sem, to, whole=False):
        size = rows if whole else half_rows
        start = source * rows + part * half_rows
        there = allg.at[pl.ds(pl.multiple_of(start, half_rows), size)]
        here = there
        if source is mf:
            here = g.at[pl.ds(part * half_rows, size)]
        return pltpu.make_async_remote_copy(
            here, there, g_s.at[sem], g_r.at[sem], device_id={"feat": to}, device_id_type=MESH
        )

    if square:
        own_sends = [
            g_copy(mf, 0, 0, near), g_copy(mf, 1, 2, far),
            g_copy(mf, 1, 1, near), g_copy(mf, 0, 3, far),
        ]
        passed = [g_copy(near, 0, 4, far), g_copy(far, 1, 5, near)]
        first = [g_copy(near, 0, 0, near), g_copy(far, 1, 2, far)]
        second = [g_copy(near, 1, 1, near), g_copy(far, 0, 3, far)]
        last = [g_copy(across_both, 0, 4, far), g_copy(across_both, 1, 5, near)]
    else:
        own_sends = [g_copy(mf, 0, k, q, True) for k, q in enumerate(feat_peers)]
        passed, first, second = [], [], []
        last = [
            g_copy(lax.rem(mf + m - 1 - k, m), 0, k, mf, True) for k in range(m - 1)
        ]

    def dom_send(src, dst, send, recv, q):
        return pltpu.make_async_remote_copy(
            src, dst, send.at[q], recv.at[me], device_id={"dom": q}, device_id_type=MESH
        )

    def dom_recv(src, dst, send, recv, q):
        return pltpu.make_async_remote_copy(
            src, dst, send.at[q], recv.at[q], device_id={"dom": q}, device_id_type=MESH
        )

    for copy in own_sends:
        copy.start()
    for load in loads[:5]:
        load.wait()

    across = lax.broadcasted_iota(jnp.int32, (tile_total, tile_total), 1)
    down = lax.broadcasted_iota(jnp.int32, (tile_total, tile_total), 0)
    key = jnp.broadcast_to(dst[...] * n + slots[...], (tile_total, tile_total))
    key_row = jnp.where(across < count[0, 0], key, pairs)
    key_column = jnp.sum(jnp.where(across == down, key_row, 0), axis=1, keepdims=True)
    earlier = (key_row == key_column) & (across < down)
    rank = jnp.sum(
        jnp.where((key_row < key_column) | earlier, 1, 0), axis=1, keepdims=True
    )
    joined = jnp.max(jnp.where(earlier, 1, 0), axis=1, keepdims=True)
    here = rank == across
    tile_order_v[...] = jnp.sum(jnp.where(here, down, 0), axis=0, keepdims=True)
    joins_v[...] = jnp.sum(jnp.where(here, joined, 0), axis=0, keepdims=True)
    pair = lax.broadcasted_iota(jnp.int32, (tile_total, pairs), 1)
    upto = jnp.sum(jnp.where(key_column <= pair, 1, 0), axis=0, keepdims=True)
    found = jnp.max(jnp.where(key_column == pair, 1, 0), axis=0, keepdims=True)
    pair_end_v[...] = upto * found
    link_copies = [
        pltpu.make_async_copy(tile_order_v, tile_order, lsem.at[8]),
        pltpu.make_async_copy(joins_v, joins, lsem.at[14]),
        pltpu.make_async_copy(pair_end_v, pair_end, lsem.at[9]),
    ]
    for copy in link_copies:
        copy.start()

    def fill_meta(o, _):
        slot = lax.fori_loop(
            0, n, lambda k, acc: jnp.where(owner[0, k] == o, k, acc), jnp.int32(0), unroll=8
        )
        slot_of[o] = slot
        value = local[0, slot].astype(F32)
        meta[o] = jnp.full((16, B), value, F32).astype(BF16)
        return 0

    lax.fori_loop(0, n, fill_meta, 0)
    for q in dom_peers:
        dom_send(meta.at[q], mrec.at[me], m_s, m_r, q).start()
    mrec[me] = meta[me]

    for copy in link_copies:
        copy.wait()
    run[0] = jnp.zeros((B, B), BF16)
    for i in range(4):
        load_tiles(i).wait()

    def add_tile(t, acc):
        acc = acc * joins[0, t].astype(F32) + tbuf[tile_order[0, t]].astype(F32)
        run[t + 1] = acc.astype(BF16)
        return acc

    acc = jnp.zeros((B, B), F32)
    for i in range(4):
        acc = lax.fori_loop(i * chunk, (i + 1) * chunk, add_tile, acc, unroll=4)
        if i == 1:
            for arrived, on in zip(first, passed):
                arrived.wait_recv()
                on.start()

    def fill_owner(o, _):
        slot = slot_of[o]
        for d in range(vb):
            adj[d * B : (d + 1) * B, pl.ds(pl.multiple_of(o * B, B), B)] = run[
                pair_end[0, d * n + slot]
            ]
        return 0

    lax.fori_loop(0, n, fill_owner, 0)

    for load in loads[5:]:
        load.wait()
    for copy in second + last:
        copy.wait_recv()
    spread[...] = jnp.dot(w[...], allg[...], preferred_element_type=F32).astype(BF16)

    half = n // 2
    def p_copy(h, q, sending):
        recv = p_r.at[h * n + (me if sending else q)]
        return pltpu.make_async_remote_copy(
            pbuf.at[h, q], prec.at[h, me if sending else q], p_s.at[h * n + q], recv,
            device_id={"dom": q}, device_id_type=MESH,
        )

    gmrec = (gmrec0, gmrec1)

    def b_copy(h, q, sending):
        recv = b_r.at[h * n + (me if sending else q)]
        return pltpu.make_async_remote_copy(
            msend.at[h, q], gmrec[h].at[me if sending else q], b_s.at[h * n + q], recv,
            device_id={"dom": q}, device_id_type=MESH,
        )

    order = []
    for i in range(half):
        c = lax.rem(me // 2 + 1 + i, half)
        columns = pl.ds(pl.multiple_of(c * 2 * B, 2 * B), 2 * B)
        part = jnp.dot(spread[...], adj[:, columns], preferred_element_type=F32).astype(BF16)
        for h in range(2):
            pbuf[h, 2 * c] = part[h * half_rows : (h + 1) * half_rows, :B]
            pbuf[h, 2 * c + 1] = part[h * half_rows : (h + 1) * half_rows, B:]
        targets = (2 * c, 2 * c + 1) if i < half - 1 else (mate,)
        for q in targets:
            p_copy(0, q, True).start()
            order.append(q)
    for q in order:
        p_copy(1, q, True).start()
    for h in range(2):
        prec[h, me] = pbuf[h, me]

    wgrad = lax.dot_general(
        s[...], allg[...], (((1,), (1,)), ((), ())), preferred_element_type=F32
    )
    if scatter:
        wrows = rows // n
        wpart[...] = wgrad.astype(BF16)

        def span(ref, start, size):
            return ref.at[pl.ds(pl.multiple_of(start, wrows), size)]

        def piece(q):
            return (lax.rem(q, 2) * half + q // 2) * wrows

        swap = pltpu.make_async_remote_copy(
            span(wpart, (1 - core) * half * wrows, half * wrows), wmate,
            x_sem.at[0], x_sem.at[1], device_id={"dom": mate}, device_id_type=MESH,
        )
        swap.start()
    else:
        wg[...] = wgrad
        flush_wg = pltpu.make_async_copy(wg, wg_out, lsem.at[10])
        flush_wg.start()

    for q in dom_peers:
        dom_recv(meta.at[q], mrec.at[q], m_s, m_r, q).wait_recv()
    rc = min(32, half_rows)

    def sum_rows(h, r, _):
        here = pl.ds(pl.multiple_of(r * rc, rc), rc)
        there = pl.ds(pl.multiple_of(h * half_rows + r * rc, rc), rc)
        pick = [mrec[p, 0:1, :].astype(F32) for p in range(n)]
        terms = [prec[h, p, here, :].astype(F32) for p in range(n)]
        back = [jnp.zeros((rc, B), F32) for _ in range(n)]
        for b in range(vb):
            hot = [jnp.where(pick[p] == b, 1.0, 0.0) for p in range(n)]
            total = terms[0] * hot[0]
            for p in range(1, n):
                total = total + terms[p] * hot[p]
            node = total.astype(BF16)
            gn[there, b * B : (b + 1) * B] = node
            node = node.astype(F32)
            back = [back[p] + node * hot[p] for p in range(n)]
        for p in range(n):
            msend[h, p, here, :] = back[p].astype(BF16)
        return 0

    for h in range(2):
        for q in order:
            p_copy(h, q, False).wait_recv()
        lax.fori_loop(0, half_rows // rc, functools.partial(sum_rows, h), 0)
        for q in order:
            b_copy(h, q, True).start()
        gmrec[h][me] = msend[h, me]
        if scatter and h == 0:
            swap.wait()
            mine = wpart[pl.ds(pl.multiple_of(core * half * wrows, wrows), half * wrows), :]
            wsend[...] = (mine.astype(F32) + wmate[...].astype(F32)).astype(BF16)
            for q in line_peers:
                dom_send(span(wsend, q // 2 * wrows, wrows), wrec.at[me // 2], ws_s, ws_r, q).start()
            wrec[me // 2] = wsend[pl.ds(pl.multiple_of(me // 2 * wrows, wrows), wrows), :]
    flush_gn = pltpu.make_async_copy(gn, gn_out, lsem.at[11])
    flush_gn.start()
    if scatter:
        for q in line_peers:
            dom_recv(span(wsend, q // 2 * wrows, wrows), wrec.at[q // 2], ws_s, ws_r, q).wait_recv()
        total = wrec[0].astype(F32)
        for p in range(1, half):
            total = total + wrec[p].astype(F32)
        wsum[...] = total.astype(BF16)
        for q in line_peers:
            dom_send(wsum, span(wg, piece(me), wrows), wg_s, wg_r, q).start()
        wg[pl.ds(pl.multiple_of(piece(me), wrows), wrows), :] = wsum[...]
        for q in line_peers:
            dom_recv(wsum, span(wg, piece(q), wrows), wg_s, wg_r, q).wait_recv()
        kept = span(wg, core * half * wrows, half * wrows)
        give = pltpu.make_async_remote_copy(
            kept, kept, x_sem.at[2], x_sem.at[3],
            device_id={"dom": mate}, device_id_type=MESH,
        )
        give.start()

    def place(h, slot, _):
        gm[h * half_rows : (h + 1) * half_rows, pl.ds(pl.multiple_of(slot * B, B), B)] = gmrec[h][
            owner[0, slot]
        ]
        return 0

    flush_gm = []
    for h in range(2):
        for q in order:
            b_copy(h, q, False).wait_recv()
        lax.fori_loop(0, n, functools.partial(place, h), 0, unroll=4)
        part = pl.ds(h * half_rows, half_rows)
        flush_gm.append(pltpu.make_async_copy(gm.at[part], gm_out.at[part], lsem.at[12 + h]))
        flush_gm[h].start()

    if scatter:
        give.wait()
        flush_wg = pltpu.make_async_copy(wg, wg_out, lsem.at[10])
        flush_wg.start()
    for copy in own_sends + passed:
        copy.wait_send()
    for q in dom_peers:
        dom_send(meta.at[q], mrec.at[me], m_s, m_r, q).wait_send()
        for h in range(2):
            p_copy(h, q, True).wait_send()
            b_copy(h, q, True).wait_send()
    if scatter:
        for q in line_peers:
            dom_send(span(wsend, q // 2 * wrows, wrows), wrec.at[me // 2], ws_s, ws_r, q).wait_send()
            dom_send(wsum, span(wg, piece(me), wrows), wg_s, wg_r, q).wait_send()
    flush_gn.wait()
    for copy in flush_gm:
        copy.wait()
    flush_wg.wait()


def finish(gn, gm, wg, gn_out, gm_out, wg_out, gn_v, gm_v, narrow, wide, sem):
    pairs = ((wg, narrow, wide, wg_out), (gm, gm_v, gm_v, gm_out), (gn, gn_v, gn_v, gn_out))
    loads = [pltpu.make_async_copy(p[0], p[1], sem.at[k]) for k, p in enumerate(pairs)]
    stores = [pltpu.make_async_copy(p[2], p[3], sem.at[3 + k]) for k, p in enumerate(pairs)]
    for load in loads:
        load.start()
    loads[0].wait()
    wide[...] = narrow[...].astype(F32)
    stores[0].start()
    for k in (1, 2):
        loads[k].wait()
        stores[k].start()
    for store in stores:
        store.wait()


def body(
    n, m,
    grad_out, saved_agg, weight, tile_values, tile_dst, tile_slot, tile_count,
    mirror_owner, mirror_local,
):
    rows, vertices = grad_out.shape
    features = weight.shape[1]
    vb = vertices // B
    tile_total = tile_values.shape[0]
    scatter = rows % (16 * n) == 0
    wrows = max(rows // n, 16)

    hbm = pl.BlockSpec(memory_space=pltpu.HBM)
    int_rows = functools.partial(pltpu.VMEM, dtype=jnp.int32)
    int_smem = functools.partial(pltpu.SMEM, dtype=jnp.int32)
    pairs = vb * n
    dma = pltpu.SemaphoreType.DMA
    wg_type = BF16 if scatter else F32
    gn, gm, wg = pl.pallas_call(
        functools.partial(kernel, n, m, vb, scatter),
        out_shape=(
            jax.ShapeDtypeStruct((rows, vertices), BF16),
            jax.ShapeDtypeStruct((rows, n * B), BF16),
            jax.ShapeDtypeStruct((rows, features), wg_type),
        ),
        in_specs=[hbm] * 9,
        out_specs=(hbm, hbm, hbm),
        scratch_shapes=[
            int_rows((1, tile_total)),
            int_rows((1, tile_total)),
            int_smem((1, 1)),
            int_smem((1, n)),
            int_smem((1, n)),
            pltpu.VMEM((rows, vertices), BF16),
            pltpu.VMEM((rows, features), BF16),
            pltpu.VMEM((tile_total, B, B), BF16),
            int_rows((1, tile_total)),
            int_rows((1, tile_total)),
            int_rows((1, pairs)),
            int_smem((1, tile_total)),
            int_smem((1, tile_total)),
            int_smem((1, pairs)),
            int_smem((n,)),
            pltpu.VMEM((tile_total + 1, B, B), BF16),
            pltpu.VMEM((vertices, n * B), BF16),
            pltpu.VMEM((features, vertices), BF16),
            pltpu.VMEM((rows, vertices), BF16),
            pltpu.VMEM((n, 16, B), BF16),
            pltpu.VMEM((n, 16, B), BF16),
            pltpu.VMEM((2, n, rows // 2, B), BF16),
            pltpu.VMEM((2, n, rows // 2, B), BF16),
            pltpu.VMEM((2, n, rows // 2, B), BF16),
            pltpu.VMEM((n, rows // 2, B), BF16),
            pltpu.VMEM((n, rows // 2, B), BF16),
            pltpu.VMEM((rows, vertices), BF16),
            pltpu.VMEM((rows, n * B), BF16),
            pltpu.VMEM((rows, features), wg_type),
            pltpu.VMEM((rows, features), BF16),
            pltpu.VMEM((wrows * n // 2, features), BF16),
            pltpu.VMEM((wrows * n // 2, features), BF16),
            pltpu.VMEM((n // 2, wrows, features), BF16),
            pltpu.VMEM((wrows, features), BF16),
            dma((15,)),
            dma((4,)),
            dma((max(m, 6),)), dma((max(m, 6),)),
            dma((n,)), dma((n,)),
            dma((2 * n,)), dma((2 * n,)),
            dma((2 * n,)), dma((2 * n,)),
            dma((n,)), dma((n,)),
            dma((n,)), dma((n,)),
            dma((4,)),
        ],
        compiler_params=pltpu.CompilerParams(
            collective_id=0, has_side_effects=True, vmem_limit_bytes=62 * 1024 * 1024
        ),
        cost_estimate=pl.CostEstimate(
            flops=2 * rows * vertices * (2 * features + n * B),
            bytes_accessed=2 * tile_total * B * B + 8 * rows * vertices,
            transcendentals=0,
        ),
    )(
        tile_dst.reshape(1, -1), tile_slot.reshape(1, -1), tile_count.reshape(1, 1),
        mirror_owner, mirror_local, grad_out, saved_agg, weight, tile_values,
    )
    if scatter:
        return pl.pallas_call(
            finish,
            out_shape=(
                jax.ShapeDtypeStruct(gn.shape, BF16),
                jax.ShapeDtypeStruct(gm.shape, BF16),
                jax.ShapeDtypeStruct(wg.shape, F32),
            ),
            in_specs=[hbm] * 3,
            out_specs=(hbm, hbm, hbm),
            scratch_shapes=[
                pltpu.VMEM(gn.shape, BF16), pltpu.VMEM(gm.shape, BF16),
                pltpu.VMEM(wg.shape, BF16), pltpu.VMEM(wg.shape, F32), dma((6,)),
            ],
        )(gn, gm, wg)
    else:
        wg = lax.psum(wg, "dom")
    return gn, gm, wg


def solution(mesh):
    in_specs = (
        P("feat", "dom"),
        P("feat", "dom"),
        P("feat", None),
        P("dom", None, None),
        P("dom"),
        P("dom"),
        P("dom"),
        P("dom", None),
        P("dom", None),
    )
    out_specs = (P("feat", "dom"), P("feat", "dom"), P("feat", None))
    return jax.shard_map(
        functools.partial(body, mesh.shape["dom"], mesh.shape["feat"]),
        mesh=mesh, in_specs=in_specs, out_specs=out_specs, check_vma=False,
    )
```

```python
import functools

import jax
import jax.numpy as jnp
from jax import lax
from jax.experimental import pallas as pl
from jax.experimental.pallas import tpu as pltpu
from jax.sharding import PartitionSpec as P

MESH = pl.DeviceIdType.MESH
B = 128
F32 = jnp.float32
BF16 = jnp.bfloat16


def kernel(
    n, m, vb, scatter, dst_hbm, slot_hbm, count_hbm, owner_hbm, local_hbm, g, s_hbm, w_hbm, tiles,
    gn_out, gm_out, wg_out,
    dst, slots, count, owner, local, s, w, tbuf, tile_order_v, joins_v, pair_end_v, tile_order,
    joins, pair_end,
    slot_of, run, adj, allg, spread, meta, mrec, pbuf, prec, msend, gmrec0, gmrec1, gn, gm, wg,
    wpart, wmate, wsend, wrec, wsum,
    lsem, tsem, g_s, g_r, m_s, m_r, p_s, p_r, b_s, b_r, ws_s, ws_r, wg_s, wg_r, x_sem,
):
    me = lax.axis_index("dom")
    mf = lax.axis_index("feat")
    rows = g.shape[0]
    tile_total = tiles.shape[0]
    pairs = vb * n
    chunk = tile_total // 4
    dom_peers = [lax.rem(me + k, n) for k in range(1, n)]
    feat_peers = [lax.rem(mf + k, m) for k in range(1, m)]
    core = lax.rem(me, 2)
    mate = me + 1 - 2 * core
    line_peers = [lax.rem(me + 2 * k, n) for k in range(1, n // 2)]

    def load_tiles(i):
        return pltpu.make_async_copy(
            tiles.at[pl.ds(i * chunk, chunk)], tbuf.at[pl.ds(i * chunk, chunk)], tsem.at[i]
        )

    my_rows = pl.ds(pl.multiple_of(mf * rows, rows), rows)
    loads = [
        pltpu.make_async_copy(a, b, lsem.at[i])
        for i, (a, b) in enumerate(
            [(dst_hbm, dst), (slot_hbm, slots), (count_hbm, count), (owner_hbm, owner),
             (local_hbm, local), (w_hbm, w), (s_hbm, s), (g, allg.at[my_rows])]
        )
    ]
    for load in loads:
        load.start()
    for i in range(4):
        load_tiles(i).start()

    barrier = pltpu.get_barrier_semaphore()
    for q in dom_peers:
        pl.semaphore_signal(barrier, inc=1, device_id={"dom": q}, device_id_type=MESH)
    for q in feat_peers:
        pl.semaphore_signal(barrier, inc=1, device_id={"feat": q}, device_id_type=MESH)
    pl.semaphore_wait(barrier, n + m - 2)

    half_rows = rows // 2
    square = m == 4
    near = mf + 1 - 2 * lax.rem(mf, 2)
    far = lax.rem(mf + 2, 4)
    across_both = lax.rem(near + 2, 4)

    def g_copy(source, part, sem, to, whole=False):
        size = rows if whole else half_rows
        start = source * rows + part * half_rows
        there = allg.at[pl.ds(pl.multiple_of(start, half_rows), size)]
        here = there
        if source is mf:
            here = g.at[pl.ds(part * half_rows, size)]
        return pltpu.make_async_remote_copy(
            here, there, g_s.at[sem], g_r.at[sem], device_id={"feat": to}, device_id_type=MESH
        )

    if square:
        own_sends = [
            g_copy(mf, 0, 0, near), g_copy(mf, 1, 2, far),
            g_copy(mf, 1, 1, near), g_copy(mf, 0, 3, far),
        ]
        passed = [g_copy(near, 0, 4, far), g_copy(far, 1, 5, near)]
        first = [g_copy(near, 0, 0, near), g_copy(far, 1, 2, far)]
        second = [g_copy(near, 1, 1, near), g_copy(far, 0, 3, far)]
        last = [g_copy(across_both, 0, 4, far), g_copy(across_both, 1, 5, near)]
    else:
        own_sends = [g_copy(mf, 0, k, q, True) for k, q in enumerate(feat_peers)]
        passed, first, second = [], [], []
        last = [
            g_copy(lax.rem(mf + m - 1 - k, m), 0, k, mf, True) for k in range(m - 1)
        ]

    def dom_send(src, dst, send, recv, q):
        return pltpu.make_async_remote_copy(
            src, dst, send.at[q], recv.at[me], device_id={"dom": q}, device_id_type=MESH
        )

    def dom_recv(src, dst, send, recv, q):
        return pltpu.make_async_remote_copy(
            src, dst, send.at[q], recv.at[q], device_id={"dom": q}, device_id_type=MESH
        )

    for copy in own_sends:
        copy.start()
    for load in loads[:5]:
        load.wait()

    across = lax.broadcasted_iota(jnp.int32, (tile_total, tile_total), 1)
    down = lax.broadcasted_iota(jnp.int32, (tile_total, tile_total), 0)
    key = jnp.broadcast_to(dst[...] * n + slots[...], (tile_total, tile_total))
    key_row = jnp.where(across < count[0, 0], key, pairs)
    key_column = jnp.sum(jnp.where(across == down, key_row, 0), axis=1, keepdims=True)
    earlier = (key_row == key_column) & (across < down)
    rank = jnp.sum(
        jnp.where((key_row < key_column) | earlier, 1, 0), axis=1, keepdims=True
    )
    joined = jnp.max(jnp.where(earlier, 1, 0), axis=1, keepdims=True)
    here = rank == across
    tile_order_v[...] = jnp.sum(jnp.where(here, down, 0), axis=0, keepdims=True)
    joins_v[...] = jnp.sum(jnp.where(here, joined, 0), axis=0, keepdims=True)
    pair = lax.broadcasted_iota(jnp.int32, (tile_total, pairs), 1)
    upto = jnp.sum(jnp.where(key_column <= pair, 1, 0), axis=0, keepdims=True)
    found = jnp.max(jnp.where(key_column == pair, 1, 0), axis=0, keepdims=True)
    pair_end_v[...] = upto * found
    link_copies = [
        pltpu.make_async_copy(tile_order_v, tile_order, lsem.at[8]),
        pltpu.make_async_copy(joins_v, joins, lsem.at[14]),
        pltpu.make_async_copy(pair_end_v, pair_end, lsem.at[9]),
    ]
    for copy in link_copies:
        copy.start()

    def fill_meta(o, _):
        slot = lax.fori_loop(
            0, n, lambda k, acc: jnp.where(owner[0, k] == o, k, acc), jnp.int32(0), unroll=8
        )
        slot_of[o] = slot
        value = local[0, slot].astype(F32)
        meta[o] = jnp.full((16, B), value, F32).astype(BF16)
        return 0

    lax.fori_loop(0, n, fill_meta, 0)
    for q in dom_peers:
        dom_send(meta.at[q], mrec.at[me], m_s, m_r, q).start()
    mrec[me] = meta[me]

    for copy in link_copies:
        copy.wait()
    run[0] = jnp.zeros((B, B), BF16)
    for i in range(4):
        load_tiles(i).wait()

    def add_tile(t, acc):
        acc = acc * joins[0, t].astype(F32) + tbuf[tile_order[0, t]].astype(F32)
        run[t + 1] = acc.astype(BF16)
        return acc

    acc = jnp.zeros((B, B), F32)
    for i in range(4):
        acc = lax.fori_loop(i * chunk, (i + 1) * chunk, add_tile, acc, unroll=4)
        if i == 1:
            for arrived, on in zip(first, passed):
                arrived.wait_recv()
                on.start()

    def fill_owner(o, _):
        slot = slot_of[o]
        for d in range(vb):
            adj[d * B : (d + 1) * B, pl.ds(pl.multiple_of(o * B, B), B)] = run[
                pair_end[0, d * n + slot]
            ]
        return 0

    lax.fori_loop(0, n, fill_owner, 0)

    for load in loads[5:]:
        load.wait()

    def piece_rows(source):
        return pl.ds(pl.multiple_of(source * rows, rows), rows)

    def back_part(source):
        here = piece_rows(source)
        return jnp.dot(w[:, here], allg[here, :], preferred_element_type=F32)

    def wgrad_part(source):
        here = piece_rows(source)
        value = lax.dot_general(
            s[...], allg[here, :], (((1,), (1,)), ((), ())), preferred_element_type=F32
        )
        wpart[:, here] = value.astype(BF16)

    pieces = square and scatter and rows % B == 0
    if pieces:
        back = back_part(mf)
        wgrad_part(mf)
        for copy in second:
            copy.wait_recv()
        back = back + back_part(near) + back_part(far)
        wgrad_part(near)
        wgrad_part(far)
        for copy in last:
            copy.wait_recv()
        spread[...] = (back + back_part(across_both)).astype(BF16)
    else:
        for copy in second + last:
            copy.wait_recv()
        spread[...] = jnp.dot(w[...], allg[...], preferred_element_type=F32).astype(BF16)

    half = n // 2
    def p_copy(h, q, sending):
        recv = p_r.at[h * n + (me if sending else q)]
        return pltpu.make_async_remote_copy(
            pbuf.at[h, q], prec.at[h, me if sending else q], p_s.at[h * n + q], recv,
            device_id={"dom": q}, device_id_type=MESH,
        )

    gmrec = (gmrec0, gmrec1)

    def b_copy(h, q, sending):
        recv = b_r.at[h * n + (me if sending else q)]
        return pltpu.make_async_remote_copy(
            msend.at[h, q], gmrec[h].at[me if sending else q], b_s.at[h * n + q], recv,
            device_id={"dom": q}, device_id_type=MESH,
        )

    order = []
    for i in range(half):
        c = lax.rem(me // 2 + 1 + i, half)
        columns = pl.ds(pl.multiple_of(c * 2 * B, 2 * B), 2 * B)
        part = jnp.dot(spread[...], adj[:, columns], preferred_element_type=F32).astype(BF16)
        for h in range(2):
            pbuf[h, 2 * c] = part[h * half_rows : (h + 1) * half_rows, :B]
            pbuf[h, 2 * c + 1] = part[h * half_rows : (h + 1) * half_rows, B:]
        targets = (2 * c, 2 * c + 1) if i < half - 1 else (mate,)
        for q in targets:
            p_copy(0, q, True).start()
            order.append(q)
    for q in order:
        p_copy(1, q, True).start()
    for h in range(2):
        prec[h, me] = pbuf[h, me]

    if pieces:
        wgrad_part(across_both)
    else:
        wgrad = lax.dot_general(
            s[...], allg[...], (((1,), (1,)), ((), ())), preferred_element_type=F32
        )
    if scatter:
        wrows = rows // n
        if not pieces:
            wpart[...] = wgrad.astype(BF16)

        def span(ref, start, size):
            return ref.at[pl.ds(pl.multiple_of(start, wrows), size)]

        def piece(q):
            return (lax.rem(q, 2) * half + q // 2) * wrows

        swap = pltpu.make_async_remote_copy(
            span(wpart, (1 - core) * half * wrows, half * wrows), wmate,
            x_sem.at[0], x_sem.at[1], device_id={"dom": mate}, device_id_type=MESH,
        )
        swap.start()
    else:
        wg[...] = wgrad
        flush_wg = pltpu.make_async_copy(wg, wg_out, lsem.at[10])
        flush_wg.start()

    for q in dom_peers:
        dom_recv(meta.at[q], mrec.at[q], m_s, m_r, q).wait_recv()
    rc = min(32, half_rows)

    def sum_rows(h, r, _):
        here = pl.ds(pl.multiple_of(r * rc, rc), rc)
        there = pl.ds(pl.multiple_of(h * half_rows + r * rc, rc), rc)
        pick = [mrec[p, 0:1, :].astype(F32) for p in range(n)]
        terms = [prec[h, p, here, :].astype(F32) for p in range(n)]
        back = [jnp.zeros((rc, B), F32) for _ in range(n)]
        for b in range(vb):
            hot = [jnp.where(pick[p] == b, 1.0, 0.0) for p in range(n)]
            total = terms[0] * hot[0]
            for p in range(1, n):
                total = total + terms[p] * hot[p]
            node = total.astype(BF16)
            gn[there, b * B : (b + 1) * B] = node
            node = node.astype(F32)
            back = [back[p] + node * hot[p] for p in range(n)]
        for p in range(n):
            msend[h, p, here, :] = back[p].astype(BF16)
        return 0

    for h in range(2):
        for q in order:
            p_copy(h, q, False).wait_recv()
        lax.fori_loop(0, half_rows // rc, functools.partial(sum_rows, h), 0)
        for q in order:
            b_copy(h, q, True).start()
        gmrec[h][me] = msend[h, me]
        if scatter and h == 0:
            swap.wait()
            mine = wpart[pl.ds(pl.multiple_of(core * half * wrows, wrows), half * wrows), :]
            wsend[...] = (mine.astype(F32) + wmate[...].astype(F32)).astype(BF16)
            for q in line_peers:
                dom_send(span(wsend, q // 2 * wrows, wrows), wrec.at[me // 2], ws_s, ws_r, q).start()
            wrec[me // 2] = wsend[pl.ds(pl.multiple_of(me // 2 * wrows, wrows), wrows), :]
    flush_gn = pltpu.make_async_copy(gn, gn_out, lsem.at[11])
    flush_gn.start()
    if scatter:
        for q in line_peers:
            dom_recv(span(wsend, q // 2 * wrows, wrows), wrec.at[q // 2], ws_s, ws_r, q).wait_recv()
        total = wrec[0].astype(F32)
        for p in range(1, half):
            total = total + wrec[p].astype(F32)
        wsum[...] = total.astype(BF16)
        for q in line_peers:
            dom_send(wsum, span(wg, piece(me), wrows), wg_s, wg_r, q).start()
        wg[pl.ds(pl.multiple_of(piece(me), wrows), wrows), :] = wsum[...]
        for q in line_peers:
            dom_recv(wsum, span(wg, piece(q), wrows), wg_s, wg_r, q).wait_recv()
        kept = span(wg, core * half * wrows, half * wrows)
        give = pltpu.make_async_remote_copy(
            kept, kept, x_sem.at[2], x_sem.at[3],
            device_id={"dom": mate}, device_id_type=MESH,
        )
        give.start()

    def place(h, slot, _):
        gm[h * half_rows : (h + 1) * half_rows, pl.ds(pl.multiple_of(slot * B, B), B)] = gmrec[h][
            owner[0, slot]
        ]
        return 0

    flush_gm = []
    for h in range(2):
        for q in order:
            b_copy(h, q, False).wait_recv()
        lax.fori_loop(0, n, functools.partial(place, h), 0, unroll=4)
        part = pl.ds(h * half_rows, half_rows)
        flush_gm.append(pltpu.make_async_copy(gm.at[part], gm_out.at[part], lsem.at[12 + h]))
        flush_gm[h].start()

    if scatter:
        give.wait()
        flush_wg = pltpu.make_async_copy(wg, wg_out, lsem.at[10])
        flush_wg.start()
    for copy in own_sends + passed:
        copy.wait_send()
    for q in dom_peers:
        dom_send(meta.at[q], mrec.at[me], m_s, m_r, q).wait_send()
        for h in range(2):
            p_copy(h, q, True).wait_send()
            b_copy(h, q, True).wait_send()
    if scatter:
        for q in line_peers:
            dom_send(span(wsend, q // 2 * wrows, wrows), wrec.at[me // 2], ws_s, ws_r, q).wait_send()
            dom_send(wsum, span(wg, piece(me), wrows), wg_s, wg_r, q).wait_send()
    flush_gn.wait()
    for copy in flush_gm:
        copy.wait()
    flush_wg.wait()


def finish(gn, gm, wg, gn_out, gm_out, wg_out, gn_v, gm_v, narrow, wide, sem):
    pairs = ((wg, narrow, wide, wg_out), (gm, gm_v, gm_v, gm_out), (gn, gn_v, gn_v, gn_out))
    loads = [pltpu.make_async_copy(p[0], p[1], sem.at[k]) for k, p in enumerate(pairs)]
    stores = [pltpu.make_async_copy(p[2], p[3], sem.at[3 + k]) for k, p in enumerate(pairs)]
    for load in loads:
        load.start()
    loads[0].wait()
    wide[...] = narrow[...].astype(F32)
    stores[0].start()
    for k in (1, 2):
        loads[k].wait()
        stores[k].start()
    for store in stores:
        store.wait()


def body(
    n, m,
    grad_out, saved_agg, weight, tile_values, tile_dst, tile_slot, tile_count,
    mirror_owner, mirror_local,
):
    rows, vertices = grad_out.shape
    features = weight.shape[1]
    vb = vertices // B
    tile_total = tile_values.shape[0]
    scatter = rows % (16 * n) == 0
    wrows = max(rows // n, 16)

    hbm = pl.BlockSpec(memory_space=pltpu.HBM)
    int_rows = functools.partial(pltpu.VMEM, dtype=jnp.int32)
    int_smem = functools.partial(pltpu.SMEM, dtype=jnp.int32)
    pairs = vb * n
    dma = pltpu.SemaphoreType.DMA
    wg_type = BF16 if scatter else F32
    gn, gm, wg = pl.pallas_call(
        functools.partial(kernel, n, m, vb, scatter),
        out_shape=(
            jax.ShapeDtypeStruct((rows, vertices), BF16),
            jax.ShapeDtypeStruct((rows, n * B), BF16),
            jax.ShapeDtypeStruct((rows, features), wg_type),
        ),
        in_specs=[hbm] * 9,
        out_specs=(hbm, hbm, hbm),
        scratch_shapes=[
            int_rows((1, tile_total)),
            int_rows((1, tile_total)),
            int_smem((1, 1)),
            int_smem((1, n)),
            int_smem((1, n)),
            pltpu.VMEM((rows, vertices), BF16),
            pltpu.VMEM((rows, features), BF16),
            pltpu.VMEM((tile_total, B, B), BF16),
            int_rows((1, tile_total)),
            int_rows((1, tile_total)),
            int_rows((1, pairs)),
            int_smem((1, tile_total)),
            int_smem((1, tile_total)),
            int_smem((1, pairs)),
            int_smem((n,)),
            pltpu.VMEM((tile_total + 1, B, B), BF16),
            pltpu.VMEM((vertices, n * B), BF16),
            pltpu.VMEM((features, vertices), BF16),
            pltpu.VMEM((rows, vertices), BF16),
            pltpu.VMEM((n, 16, B), BF16),
            pltpu.VMEM((n, 16, B), BF16),
            pltpu.VMEM((2, n, rows // 2, B), BF16),
            pltpu.VMEM((2, n, rows // 2, B), BF16),
            pltpu.VMEM((2, n, rows // 2, B), BF16),
            pltpu.VMEM((n, rows // 2, B), BF16),
            pltpu.VMEM((n, rows // 2, B), BF16),
            pltpu.VMEM((rows, vertices), BF16),
            pltpu.VMEM((rows, n * B), BF16),
            pltpu.VMEM((rows, features), wg_type),
            pltpu.VMEM((rows, features), BF16),
            pltpu.VMEM((wrows * n // 2, features), BF16),
            pltpu.VMEM((wrows * n // 2, features), BF16),
            pltpu.VMEM((n // 2, wrows, features), BF16),
            pltpu.VMEM((wrows, features), BF16),
            dma((15,)),
            dma((4,)),
            dma((max(m, 6),)), dma((max(m, 6),)),
            dma((n,)), dma((n,)),
            dma((2 * n,)), dma((2 * n,)),
            dma((2 * n,)), dma((2 * n,)),
            dma((n,)), dma((n,)),
            dma((n,)), dma((n,)),
            dma((4,)),
        ],
        compiler_params=pltpu.CompilerParams(
            collective_id=0, has_side_effects=True, vmem_limit_bytes=62 * 1024 * 1024
        ),
        cost_estimate=pl.CostEstimate(
            flops=2 * rows * vertices * (2 * features + n * B),
            bytes_accessed=2 * tile_total * B * B + 8 * rows * vertices,
            transcendentals=0,
        ),
    )(
        tile_dst.reshape(1, -1), tile_slot.reshape(1, -1), tile_count.reshape(1, 1),
        mirror_owner, mirror_local, grad_out, saved_agg, weight, tile_values,
    )
    if scatter:
        return pl.pallas_call(
            finish,
            out_shape=(
                jax.ShapeDtypeStruct(gn.shape, BF16),
                jax.ShapeDtypeStruct(gm.shape, BF16),
                jax.ShapeDtypeStruct(wg.shape, F32),
            ),
            in_specs=[hbm] * 3,
            out_specs=(hbm, hbm, hbm),
            scratch_shapes=[
                pltpu.VMEM(gn.shape, BF16), pltpu.VMEM(gm.shape, BF16),
                pltpu.VMEM(wg.shape, BF16), pltpu.VMEM(wg.shape, F32), dma((6,)),
            ],
        )(gn, gm, wg)
    else:
        wg = lax.psum(wg, "dom")
    return gn, gm, wg


def solution(mesh):
    in_specs = (
        P("feat", "dom"),
        P("feat", "dom"),
        P("feat", None),
        P("dom", None, None),
        P("dom"),
        P("dom"),
        P("dom"),
        P("dom", None),
        P("dom", None),
    )
    out_specs = (P("feat", "dom"), P("feat", "dom"), P("feat", None))
    return jax.shard_map(
        functools.partial(body, mesh.shape["dom"], mesh.shape["feat"]),
        mesh=mesh, in_specs=in_specs, out_specs=out_specs, check_vma=False,
    )
```

```python
import functools

import jax
import jax.numpy as jnp
from jax import lax
from jax.experimental import pallas as pl
from jax.experimental.pallas import tpu as pltpu
from jax.sharding import PartitionSpec as P

MESH = pl.DeviceIdType.MESH
B = 128
F32 = jnp.float32
BF16 = jnp.bfloat16


def kernel(
    n, m, vb, scatter, dst_hbm, slot_hbm, count_hbm, owner_hbm, local_hbm, g, s_hbm, w_hbm, tiles,
    gn_out, gm_out, wg_out,
    dst, slots, count, owner, local, s, w, tbuf, tile_order_v, joins_v, pair_end_v, tile_order,
    joins, pair_end,
    slot_of, run, adj, allg, spread, meta, mrec, pbuf, prec, msend, gmrec0, gmrec1, gn, gm, wg,
    wpart, wmate, wsend, wrec, wsum,
    lsem, tsem, g_s, g_r, m_s, m_r, p_s, p_r, b_s, b_r, ws_s, ws_r, wg_s, wg_r, x_sem,
):
    me = lax.axis_index("dom")
    mf = lax.axis_index("feat")
    rows = g.shape[0]
    tile_total = tiles.shape[0]
    pairs = vb * n
    chunk = tile_total // 4
    dom_peers = [lax.rem(me + k, n) for k in range(1, n)]
    feat_peers = [lax.rem(mf + k, m) for k in range(1, m)]
    core = lax.rem(me, 2)
    mate = me + 1 - 2 * core
    line_peers = [lax.rem(me + 2 * k, n) for k in range(1, n // 2)]

    def load_tiles(i):
        return pltpu.make_async_copy(
            tiles.at[pl.ds(i * chunk, chunk)], tbuf.at[pl.ds(i * chunk, chunk)], tsem.at[i]
        )

    my_rows = pl.ds(pl.multiple_of(mf * rows, rows), rows)
    loads = [
        pltpu.make_async_copy(a, b, lsem.at[i])
        for i, (a, b) in enumerate(
            [(dst_hbm, dst), (slot_hbm, slots), (count_hbm, count), (owner_hbm, owner),
             (local_hbm, local), (w_hbm, w), (s_hbm, s), (g, allg.at[my_rows])]
        )
    ]
    for load in loads:
        load.start()
    for i in range(4):
        load_tiles(i).start()

    barrier = pltpu.get_barrier_semaphore()
    for q in dom_peers:
        pl.semaphore_signal(barrier, inc=1, device_id={"dom": q}, device_id_type=MESH)
    for q in feat_peers:
        pl.semaphore_signal(barrier, inc=1, device_id={"feat": q}, device_id_type=MESH)
    pl.semaphore_wait(barrier, n + m - 2)

    half_rows = rows // 2
    square = m == 4
    near = mf + 1 - 2 * lax.rem(mf, 2)
    far = lax.rem(mf + 2, 4)
    across_both = lax.rem(near + 2, 4)

    def g_copy(source, part, sem, to, whole=False):
        size = rows if whole else half_rows
        start = source * rows + part * half_rows
        there = allg.at[pl.ds(pl.multiple_of(start, half_rows), size)]
        here = there
        if source is mf:
            here = g.at[pl.ds(part * half_rows, size)]
        return pltpu.make_async_remote_copy(
            here, there, g_s.at[sem], g_r.at[sem], device_id={"feat": to}, device_id_type=MESH
        )

    if square:
        own_sends = [
            g_copy(mf, 0, 0, near), g_copy(mf, 1, 2, far),
            g_copy(mf, 1, 1, near), g_copy(mf, 0, 3, far),
        ]
        passed = [g_copy(near, 0, 4, far), g_copy(far, 1, 5, near)]
        first = [g_copy(near, 0, 0, near), g_copy(far, 1, 2, far)]
        second = [g_copy(near, 1, 1, near), g_copy(far, 0, 3, far)]
        last = [g_copy(across_both, 0, 4, far), g_copy(across_both, 1, 5, near)]
    else:
        own_sends = [g_copy(mf, 0, k, q, True) for k, q in enumerate(feat_peers)]
        passed, first, second = [], [], []
        last = [
            g_copy(lax.rem(mf + m - 1 - k, m), 0, k, mf, True) for k in range(m - 1)
        ]

    def dom_send(src, dst, send, recv, q):
        return pltpu.make_async_remote_copy(
            src, dst, send.at[q], recv.at[me], device_id={"dom": q}, device_id_type=MESH
        )

    def dom_recv(src, dst, send, recv, q):
        return pltpu.make_async_remote_copy(
            src, dst, send.at[q], recv.at[q], device_id={"dom": q}, device_id_type=MESH
        )

    for copy in own_sends:
        copy.start()
    for load in loads[:5]:
        load.wait()

    across = lax.broadcasted_iota(jnp.int32, (tile_total, tile_total), 1)
    down = lax.broadcasted_iota(jnp.int32, (tile_total, tile_total), 0)
    key = jnp.broadcast_to(dst[...] * n + slots[...], (tile_total, tile_total))
    key_row = jnp.where(across < count[0, 0], key, pairs)
    key_column = jnp.sum(jnp.where(across == down, key_row, 0), axis=1, keepdims=True)
    earlier = (key_row == key_column) & (across < down)
    rank = jnp.sum(
        jnp.where((key_row < key_column) | earlier, 1, 0), axis=1, keepdims=True
    )
    joined = jnp.max(jnp.where(earlier, 1, 0), axis=1, keepdims=True)
    here = rank == across
    tile_order_v[...] = jnp.sum(jnp.where(here, down, 0), axis=0, keepdims=True)
    joins_v[...] = jnp.sum(jnp.where(here, joined, 0), axis=0, keepdims=True)
    pair = lax.broadcasted_iota(jnp.int32, (tile_total, pairs), 1)
    upto = jnp.sum(jnp.where(key_column <= pair, 1, 0), axis=0, keepdims=True)
    found = jnp.max(jnp.where(key_column == pair, 1, 0), axis=0, keepdims=True)
    pair_end_v[...] = upto * found
    link_copies = [
        pltpu.make_async_copy(tile_order_v, tile_order, lsem.at[8]),
        pltpu.make_async_copy(joins_v, joins, lsem.at[14]),
        pltpu.make_async_copy(pair_end_v, pair_end, lsem.at[9]),
    ]
    for copy in link_copies:
        copy.start()

    def fill_meta(o, _):
        slot = lax.fori_loop(
            0, n, lambda k, acc: jnp.where(owner[0, k] == o, k, acc), jnp.int32(0), unroll=8
        )
        slot_of[o] = slot
        value = local[0, slot].astype(F32)
        meta[o] = jnp.full((16, B), value, F32).astype(BF16)
        return 0

    lax.fori_loop(0, n, fill_meta, 0)
    for q in dom_peers:
        dom_send(meta.at[q], mrec.at[me], m_s, m_r, q).start()
    mrec[me] = meta[me]

    for copy in link_copies:
        copy.wait()
    run[0] = jnp.zeros((B, B), BF16)
    for i in range(4):
        load_tiles(i).wait()

    def add_tile(t, acc):
        acc = acc * joins[0, t].astype(F32) + tbuf[tile_order[0, t]].astype(F32)
        run[t + 1] = acc.astype(BF16)
        return acc

    acc = jnp.zeros((B, B), F32)
    for i in range(4):
        acc = lax.fori_loop(i * chunk, (i + 1) * chunk, add_tile, acc, unroll=4)
        if i == 1:
            for arrived, on in zip(first, passed):
                arrived.wait_recv()
                on.start()

    def fill_owner(o, _):
        slot = slot_of[o]
        for d in range(vb):
            adj[d * B : (d + 1) * B, pl.ds(pl.multiple_of(o * B, B), B)] = run[
                pair_end[0, d * n + slot]
            ]
        return 0

    lax.fori_loop(0, n, fill_owner, 0)

    for load in loads[5:]:
        load.wait()

    def piece_rows(source):
        return pl.ds(pl.multiple_of(source * rows, rows), rows)

    def back_part(source):
        here = piece_rows(source)
        return jnp.dot(w[:, here], allg[here, :], preferred_element_type=F32)

    def wgrad_part(source):
        here = piece_rows(source)
        value = lax.dot_general(
            s[...], allg[here, :], (((1,), (1,)), ((), ())), preferred_element_type=F32
        )
        wpart[:, here] = value.astype(BF16)

    pieces = square and scatter and rows % B == 0
    if pieces:
        back = back_part(mf)
        wgrad_part(mf)
        for copy in second:
            copy.wait_recv()
        back = back + back_part(near) + back_part(far)
        wgrad_part(near)
        wgrad_part(far)
        for copy in last:
            copy.wait_recv()
        spread[...] = (back + back_part(across_both)).astype(BF16)
    else:
        for copy in second + last:
            copy.wait_recv()
        spread[...] = jnp.dot(w[...], allg[...], preferred_element_type=F32).astype(BF16)

    half = n // 2
    def p_copy(h, q, sending):
        recv = p_r.at[h * n + (me if sending else q)]
        return pltpu.make_async_remote_copy(
            pbuf.at[h, q], prec.at[h, me if sending else q], p_s.at[h * n + q], recv,
            device_id={"dom": q}, device_id_type=MESH,
        )

    gmrec = (gmrec0, gmrec1)

    def b_copy(h, q, sending):
        recv = b_r.at[h * n + (me if sending else q)]
        return pltpu.make_async_remote_copy(
            msend.at[h, q], gmrec[h].at[me if sending else q], b_s.at[h * n + q], recv,
            device_id={"dom": q}, device_id_type=MESH,
        )

    order = []
    for i in range(half):
        c = lax.rem(me // 2 + 1 + i, half)
        columns = pl.ds(pl.multiple_of(c * 2 * B, 2 * B), 2 * B)
        part = jnp.dot(spread[...], adj[:, columns], preferred_element_type=F32).astype(BF16)
        for h in range(2):
            pbuf[h, 2 * c] = part[h * half_rows : (h + 1) * half_rows, :B]
            pbuf[h, 2 * c + 1] = part[h * half_rows : (h + 1) * half_rows, B:]
        targets = (2 * c, 2 * c + 1) if i < half - 1 else (mate,)
        for q in targets:
            p_copy(0, q, True).start()
            order.append(q)
    for h in range(2):
        prec[h, me] = pbuf[h, me]

    if pieces:
        wgrad_part(across_both)
    else:
        wgrad = lax.dot_general(
            s[...], allg[...], (((1,), (1,)), ((), ())), preferred_element_type=F32
        )
    if scatter:
        wrows = rows // n
        if not pieces:
            wpart[...] = wgrad.astype(BF16)

        def span(ref, start, size):
            return ref.at[pl.ds(pl.multiple_of(start, wrows), size)]

        def piece(q):
            return (lax.rem(q, 2) * half + q // 2) * wrows

        swap = pltpu.make_async_remote_copy(
            span(wpart, (1 - core) * half * wrows, half * wrows), wmate,
            x_sem.at[0], x_sem.at[1], device_id={"dom": mate}, device_id_type=MESH,
        )
        swap.start()
        swap.wait()
        mine = wpart[pl.ds(pl.multiple_of(core * half * wrows, wrows), half * wrows), :]
        wsend[...] = (mine.astype(F32) + wmate[...].astype(F32)).astype(BF16)
        for q in line_peers:
            dom_send(span(wsend, q // 2 * wrows, wrows), wrec.at[me // 2], ws_s, ws_r, q).start()
        wrec[me // 2] = wsend[pl.ds(pl.multiple_of(me // 2 * wrows, wrows), wrows), :]
    else:
        wg[...] = wgrad
        flush_wg = pltpu.make_async_copy(wg, wg_out, lsem.at[10])
        flush_wg.start()

    for q in order:
        p_copy(1, q, True).start()

    for q in dom_peers:
        dom_recv(meta.at[q], mrec.at[q], m_s, m_r, q).wait_recv()
    rc = min(32, half_rows)

    def sum_rows(h, r, _):
        here = pl.ds(pl.multiple_of(r * rc, rc), rc)
        there = pl.ds(pl.multiple_of(h * half_rows + r * rc, rc), rc)
        pick = [mrec[p, 0:1, :].astype(F32) for p in range(n)]
        terms = [prec[h, p, here, :].astype(F32) for p in range(n)]
        back = [jnp.zeros((rc, B), F32) for _ in range(n)]
        for b in range(vb):
            hot = [jnp.where(pick[p] == b, 1.0, 0.0) for p in range(n)]
            total = terms[0] * hot[0]
            for p in range(1, n):
                total = total + terms[p] * hot[p]
            node = total.astype(BF16)
            gn[there, b * B : (b + 1) * B] = node
            node = node.astype(F32)
            back = [back[p] + node * hot[p] for p in range(n)]
        for p in range(n):
            msend[h, p, here, :] = back[p].astype(BF16)
        return 0

    for h in range(2):
        for q in order:
            p_copy(h, q, False).wait_recv()
        lax.fori_loop(0, half_rows // rc, functools.partial(sum_rows, h), 0)
        for q in order:
            b_copy(h, q, True).start()
        gmrec[h][me] = msend[h, me]
        if scatter and h == 0:
            for q in line_peers:
                dom_recv(
                    span(wsend, q // 2 * wrows, wrows), wrec.at[q // 2], ws_s, ws_r, q
                ).wait_recv()
            total = wrec[0].astype(F32)
            for p in range(1, half):
                total = total + wrec[p].astype(F32)
            wsum[...] = total.astype(BF16)
            for q in line_peers:
                dom_send(wsum, span(wg, piece(me), wrows), wg_s, wg_r, q).start()
            wg[pl.ds(pl.multiple_of(piece(me), wrows), wrows), :] = wsum[...]
    flush_gn = pltpu.make_async_copy(gn, gn_out, lsem.at[11])
    flush_gn.start()
    if scatter:
        for q in line_peers:
            dom_recv(wsum, span(wg, piece(q), wrows), wg_s, wg_r, q).wait_recv()
        kept = span(wg, core * half * wrows, half * wrows)
        give = pltpu.make_async_remote_copy(
            kept, kept, x_sem.at[2], x_sem.at[3],
            device_id={"dom": mate}, device_id_type=MESH,
        )
        give.start()

    def place(h, slot, _):
        gm[h * half_rows : (h + 1) * half_rows, pl.ds(pl.multiple_of(slot * B, B), B)] = gmrec[h][
            owner[0, slot]
        ]
        return 0

    flush_gm = []
    for h in range(2):
        for q in order:
            b_copy(h, q, False).wait_recv()
        lax.fori_loop(0, n, functools.partial(place, h), 0, unroll=4)
        part = pl.ds(h * half_rows, half_rows)
        flush_gm.append(pltpu.make_async_copy(gm.at[part], gm_out.at[part], lsem.at[12 + h]))
        flush_gm[h].start()

    if scatter:
        give.wait()
        flush_wg = pltpu.make_async_copy(wg, wg_out, lsem.at[10])
        flush_wg.start()
    for copy in own_sends + passed:
        copy.wait_send()
    for q in dom_peers:
        dom_send(meta.at[q], mrec.at[me], m_s, m_r, q).wait_send()
        for h in range(2):
            p_copy(h, q, True).wait_send()
            b_copy(h, q, True).wait_send()
    if scatter:
        for q in line_peers:
            dom_send(span(wsend, q // 2 * wrows, wrows), wrec.at[me // 2], ws_s, ws_r, q).wait_send()
            dom_send(wsum, span(wg, piece(me), wrows), wg_s, wg_r, q).wait_send()
    flush_gn.wait()
    for copy in flush_gm:
        copy.wait()
    flush_wg.wait()


def finish(gn, gm, wg, gn_out, gm_out, wg_out, gn_v, gm_v, narrow, wide, sem):
    pairs = ((wg, narrow, wide, wg_out), (gm, gm_v, gm_v, gm_out), (gn, gn_v, gn_v, gn_out))
    loads = [pltpu.make_async_copy(p[0], p[1], sem.at[k]) for k, p in enumerate(pairs)]
    stores = [pltpu.make_async_copy(p[2], p[3], sem.at[3 + k]) for k, p in enumerate(pairs)]
    for load in loads:
        load.start()
    loads[0].wait()
    wide[...] = narrow[...].astype(F32)
    stores[0].start()
    for k in (1, 2):
        loads[k].wait()
        stores[k].start()
    for store in stores:
        store.wait()


def body(
    n, m,
    grad_out, saved_agg, weight, tile_values, tile_dst, tile_slot, tile_count,
    mirror_owner, mirror_local,
):
    rows, vertices = grad_out.shape
    features = weight.shape[1]
    vb = vertices // B
    tile_total = tile_values.shape[0]
    scatter = rows % (16 * n) == 0
    wrows = max(rows // n, 16)

    hbm = pl.BlockSpec(memory_space=pltpu.HBM)
    int_rows = functools.partial(pltpu.VMEM, dtype=jnp.int32)
    int_smem = functools.partial(pltpu.SMEM, dtype=jnp.int32)
    pairs = vb * n
    dma = pltpu.SemaphoreType.DMA
    wg_type = BF16 if scatter else F32
    gn, gm, wg = pl.pallas_call(
        functools.partial(kernel, n, m, vb, scatter),
        out_shape=(
            jax.ShapeDtypeStruct((rows, vertices), BF16),
            jax.ShapeDtypeStruct((rows, n * B), BF16),
            jax.ShapeDtypeStruct((rows, features), wg_type),
        ),
        in_specs=[hbm] * 9,
        out_specs=(hbm, hbm, hbm),
        scratch_shapes=[
            int_rows((1, tile_total)),
            int_rows((1, tile_total)),
            int_smem((1, 1)),
            int_smem((1, n)),
            int_smem((1, n)),
            pltpu.VMEM((rows, vertices), BF16),
            pltpu.VMEM((rows, features), BF16),
            pltpu.VMEM((tile_total, B, B), BF16),
            int_rows((1, tile_total)),
            int_rows((1, tile_total)),
            int_rows((1, pairs)),
            int_smem((1, tile_total)),
            int_smem((1, tile_total)),
            int_smem((1, pairs)),
            int_smem((n,)),
            pltpu.VMEM((tile_total + 1, B, B), BF16),
            pltpu.VMEM((vertices, n * B), BF16),
            pltpu.VMEM((features, vertices), BF16),
            pltpu.VMEM((rows, vertices), BF16),
            pltpu.VMEM((n, 16, B), BF16),
            pltpu.VMEM((n, 16, B), BF16),
            pltpu.VMEM((2, n, rows // 2, B), BF16),
            pltpu.VMEM((2, n, rows // 2, B), BF16),
            pltpu.VMEM((2, n, rows // 2, B), BF16),
            pltpu.VMEM((n, rows // 2, B), BF16),
            pltpu.VMEM((n, rows // 2, B), BF16),
            pltpu.VMEM((rows, vertices), BF16),
            pltpu.VMEM((rows, n * B), BF16),
            pltpu.VMEM((rows, features), wg_type),
            pltpu.VMEM((rows, features), BF16),
            pltpu.VMEM((wrows * n // 2, features), BF16),
            pltpu.VMEM((wrows * n // 2, features), BF16),
            pltpu.VMEM((n // 2, wrows, features), BF16),
            pltpu.VMEM((wrows, features), BF16),
            dma((15,)),
            dma((4,)),
            dma((max(m, 6),)), dma((max(m, 6),)),
            dma((n,)), dma((n,)),
            dma((2 * n,)), dma((2 * n,)),
            dma((2 * n,)), dma((2 * n,)),
            dma((n,)), dma((n,)),
            dma((n,)), dma((n,)),
            dma((4,)),
        ],
        compiler_params=pltpu.CompilerParams(
            collective_id=0, has_side_effects=True, vmem_limit_bytes=62 * 1024 * 1024
        ),
        cost_estimate=pl.CostEstimate(
            flops=2 * rows * vertices * (2 * features + n * B),
            bytes_accessed=2 * tile_total * B * B + 8 * rows * vertices,
            transcendentals=0,
        ),
    )(
        tile_dst.reshape(1, -1), tile_slot.reshape(1, -1), tile_count.reshape(1, 1),
        mirror_owner, mirror_local, grad_out, saved_agg, weight, tile_values,
    )
    if scatter:
        return pl.pallas_call(
            finish,
            out_shape=(
                jax.ShapeDtypeStruct(gn.shape, BF16),
                jax.ShapeDtypeStruct(gm.shape, BF16),
                jax.ShapeDtypeStruct(wg.shape, F32),
            ),
            in_specs=[hbm] * 3,
            out_specs=(hbm, hbm, hbm),
            scratch_shapes=[
                pltpu.VMEM(gn.shape, BF16), pltpu.VMEM(gm.shape, BF16),
                pltpu.VMEM(wg.shape, BF16), pltpu.VMEM(wg.shape, F32), dma((6,)),
            ],
        )(gn, gm, wg)
    else:
        wg = lax.psum(wg, "dom")
    return gn, gm, wg


def solution(mesh):
    in_specs = (
        P("feat", "dom"),
        P("feat", "dom"),
        P("feat", None),
        P("dom", None, None),
        P("dom"),
        P("dom"),
        P("dom"),
        P("dom", None),
        P("dom", None),
    )
    out_specs = (P("feat", "dom"), P("feat", "dom"), P("feat", None))
    return jax.shard_map(
        functools.partial(body, mesh.shape["dom"], mesh.shape["feat"]),
        mesh=mesh, in_specs=in_specs, out_specs=out_specs, check_vma=False,
    )
```

```python
import functools

import jax
import jax.numpy as jnp
from jax import lax
from jax.experimental import pallas as pl
from jax.experimental.pallas import tpu as pltpu
from jax.sharding import PartitionSpec as P

MESH = pl.DeviceIdType.MESH
B = 128
F32 = jnp.float32
BF16 = jnp.bfloat16


def kernel(
    n, m, vb, scatter, dst_hbm, slot_hbm, count_hbm, owner_hbm, local_hbm, g, s_hbm, w_hbm, tiles,
    gn_out, gm_out, wg_out,
    dst, slots, count, owner, local, s, w, tbuf, tile_order_v, joins_v, pair_end_v, tile_order,
    joins, pair_end,
    slot_of, run, adj, allg, spread, meta, mrec, pbuf, prec, msend, gmrec0, gmrec1, gn, gm, wg,
    wpart, wmate, wsend, wrec, wsum,
    lsem, tsem, g_s, g_r, m_s, m_r, p_s, p_r, b_s, b_r, ws_s, ws_r, wg_s, wg_r, x_sem,
):
    me = lax.axis_index("dom")
    mf = lax.axis_index("feat")
    rows = g.shape[0]
    tile_total = tiles.shape[0]
    pairs = vb * n
    chunk = tile_total // 4
    dom_peers = [lax.rem(me + k, n) for k in range(1, n)]
    feat_peers = [lax.rem(mf + k, m) for k in range(1, m)]
    core = lax.rem(me, 2)
    mate = me + 1 - 2 * core
    line_peers = [lax.rem(me + 2 * k, n) for k in range(1, n // 2)]

    def load_tiles(i):
        return pltpu.make_async_copy(
            tiles.at[pl.ds(i * chunk, chunk)], tbuf.at[pl.ds(i * chunk, chunk)], tsem.at[i]
        )

    my_rows = pl.ds(pl.multiple_of(mf * rows, rows), rows)
    loads = [
        pltpu.make_async_copy(a, b, lsem.at[i])
        for i, (a, b) in enumerate(
            [(dst_hbm, dst), (slot_hbm, slots), (count_hbm, count), (owner_hbm, owner),
             (local_hbm, local), (w_hbm, w), (s_hbm, s), (g, allg.at[my_rows])]
        )
    ]
    for load in loads:
        load.start()
    for i in range(4):
        load_tiles(i).start()

    barrier = pltpu.get_barrier_semaphore()
    for q in dom_peers:
        pl.semaphore_signal(barrier, inc=1, device_id={"dom": q}, device_id_type=MESH)
    for q in feat_peers:
        pl.semaphore_signal(barrier, inc=1, device_id={"feat": q}, device_id_type=MESH)
    pl.semaphore_wait(barrier, n + m - 2)

    half_rows = rows // 2
    square = m == 4
    near = mf + 1 - 2 * lax.rem(mf, 2)
    far = lax.rem(mf + 2, 4)
    across_both = lax.rem(near + 2, 4)

    def g_copy(source, part, sem, to, whole=False):
        size = rows if whole else half_rows
        start = source * rows + part * half_rows
        there = allg.at[pl.ds(pl.multiple_of(start, half_rows), size)]
        here = there
        if source is mf:
            here = g.at[pl.ds(part * half_rows, size)]
        return pltpu.make_async_remote_copy(
            here, there, g_s.at[sem], g_r.at[sem], device_id={"feat": to}, device_id_type=MESH
        )

    if square:
        own_sends = [
            g_copy(mf, 0, 0, near), g_copy(mf, 1, 2, far),
            g_copy(mf, 1, 1, near), g_copy(mf, 0, 3, far),
        ]
        passed = [g_copy(near, 0, 4, far), g_copy(far, 1, 5, near)]
        first = [g_copy(near, 0, 0, near), g_copy(far, 1, 2, far)]
        second = [g_copy(near, 1, 1, near), g_copy(far, 0, 3, far)]
        last = [g_copy(across_both, 0, 4, far), g_copy(across_both, 1, 5, near)]
    else:
        own_sends = [g_copy(mf, 0, k, q, True) for k, q in enumerate(feat_peers)]
        passed, first, second = [], [], []
        last = [
            g_copy(lax.rem(mf + m - 1 - k, m), 0, k, mf, True) for k in range(m - 1)
        ]

    def dom_send(src, dst, send, recv, q):
        return pltpu.make_async_remote_copy(
            src, dst, send.at[q], recv.at[me], device_id={"dom": q}, device_id_type=MESH
        )

    def dom_recv(src, dst, send, recv, q):
        return pltpu.make_async_remote_copy(
            src, dst, send.at[q], recv.at[q], device_id={"dom": q}, device_id_type=MESH
        )

    for copy in own_sends:
        copy.start()
    for load in loads[:5]:
        load.wait()

    across = lax.broadcasted_iota(jnp.int32, (tile_total, tile_total), 1)
    down = lax.broadcasted_iota(jnp.int32, (tile_total, tile_total), 0)
    key = jnp.broadcast_to(dst[...] * n + slots[...], (tile_total, tile_total))
    key_row = jnp.where(across < count[0, 0], key, pairs)
    key_column = jnp.sum(jnp.where(across == down, key_row, 0), axis=1, keepdims=True)
    earlier = (key_row == key_column) & (across < down)
    rank = jnp.sum(
        jnp.where((key_row < key_column) | earlier, 1, 0), axis=1, keepdims=True
    )
    joined = jnp.max(jnp.where(earlier, 1, 0), axis=1, keepdims=True)
    here = rank == across
    tile_order_v[...] = jnp.sum(jnp.where(here, down, 0), axis=0, keepdims=True)
    joins_v[...] = jnp.sum(jnp.where(here, joined, 0), axis=0, keepdims=True)
    pair = lax.broadcasted_iota(jnp.int32, (tile_total, pairs), 1)
    upto = jnp.sum(jnp.where(key_column <= pair, 1, 0), axis=0, keepdims=True)
    found = jnp.max(jnp.where(key_column == pair, 1, 0), axis=0, keepdims=True)
    pair_end_v[...] = upto * found
    link_copies = [
        pltpu.make_async_copy(tile_order_v, tile_order, lsem.at[8]),
        pltpu.make_async_copy(joins_v, joins, lsem.at[14]),
        pltpu.make_async_copy(pair_end_v, pair_end, lsem.at[9]),
    ]
    for copy in link_copies:
        copy.start()

    def fill_meta(o, _):
        slot = lax.fori_loop(
            0, n, lambda k, acc: jnp.where(owner[0, k] == o, k, acc), jnp.int32(0), unroll=8
        )
        slot_of[o] = slot
        value = local[0, slot].astype(F32)
        meta[o] = jnp.full((16, B), value, F32).astype(BF16)
        return 0

    lax.fori_loop(0, n, fill_meta, 0)
    for q in dom_peers:
        dom_send(meta.at[q], mrec.at[me], m_s, m_r, q).start()
    mrec[me] = meta[me]

    for copy in link_copies:
        copy.wait()
    run[0] = jnp.zeros((B, B), BF16)
    for i in range(4):
        load_tiles(i).wait()

    def add_tile(t, acc):
        acc = acc * joins[0, t].astype(F32) + tbuf[tile_order[0, t]].astype(F32)
        run[t + 1] = acc.astype(BF16)
        return acc

    acc = jnp.zeros((B, B), F32)
    for i in range(4):
        acc = lax.fori_loop(i * chunk, (i + 1) * chunk, add_tile, acc, unroll=4)
        if i == 1:
            for arrived, on in zip(first, passed):
                arrived.wait_recv()
                on.start()

    def fill_owner(o, _):
        slot = slot_of[o]
        for d in range(vb):
            adj[d * B : (d + 1) * B, pl.ds(pl.multiple_of(o * B, B), B)] = run[
                pair_end[0, d * n + slot]
            ]
        return 0

    lax.fori_loop(0, n, fill_owner, 0)

    for load in loads[5:]:
        load.wait()

    def piece_rows(source):
        return pl.ds(pl.multiple_of(source * rows, rows), rows)

    def back_part(source):
        here = piece_rows(source)
        return jnp.dot(w[:, here], allg[here, :], preferred_element_type=F32)

    def wgrad_part(source, k):
        here = piece_rows(source)
        value = lax.dot_general(
            s[...], allg[here, :], (((1,), (1,)), ((), ())), preferred_element_type=F32
        )
        wpart[:, k * B : (k + 1) * B] = value.astype(BF16)

    pieces = square and scatter and rows % B == 0
    half = n // 2
    wrows = rows // n
    features = w.shape[1]
    groups = ((0, features - B), (features - B, B)) if pieces else ((0, 0), (0, features))

    def span(ref, start, size, g=None):
        here = pl.ds(pl.multiple_of(start, wrows), size)
        return ref.at[here] if g is None else ref.at[here, pl.ds(*groups[g])]

    def piece(q):
        return (lax.rem(q, 2) * half + q // 2) * wrows

    def swap_copy(g):
        return pltpu.make_async_remote_copy(
            span(wpart, (1 - core) * half * wrows, half * wrows, g),
            wmate.at[:, pl.ds(*groups[g])],
            x_sem.at[4 * g], x_sem.at[4 * g + 1], device_id={"dom": mate}, device_id_type=MESH,
        )

    def line_copy(g, q, sending):
        there = me // 2 if sending else q // 2
        return pltpu.make_async_remote_copy(
            span(wsend, q // 2 * wrows, wrows, g), wrec.at[there, :, pl.ds(*groups[g])],
            ws_s.at[g * n + q], ws_r.at[g * n + (me if sending else q)],
            device_id={"dom": q}, device_id_type=MESH,
        )

    def swap_start(g):
        swap_copy(g).start()

    def pair_sum(g):
        swap_copy(g).wait()
        lanes = pl.ds(*groups[g])
        mine = wpart[pl.ds(pl.multiple_of(core * half * wrows, wrows), half * wrows), lanes]
        wsend[:, lanes] = (mine.astype(F32) + wmate[:, lanes].astype(F32)).astype(BF16)
        for q in line_peers:
            line_copy(g, q, True).start()
        own = wsend[pl.ds(pl.multiple_of(me // 2 * wrows, wrows), wrows), lanes]
        wrec[me // 2, :, lanes] = own

    used_groups = (0, 1) if pieces else (1,)
    if pieces:
        back = back_part(mf)
        wgrad_part(mf, 0)
        for copy in second:
            copy.wait_recv()
        back = back + back_part(near) + back_part(far)
        wgrad_part(near, 1)
        wgrad_part(far, 2)
        swap_start(0)
        pair_sum(0)
        for copy in last:
            copy.wait_recv()
        spread[...] = (back + back_part(across_both)).astype(BF16)
    else:
        for copy in second + last:
            copy.wait_recv()
        spread[...] = jnp.dot(w[...], allg[...], preferred_element_type=F32).astype(BF16)

    def p_copy(h, q, sending):
        recv = p_r.at[h * n + (me if sending else q)]
        return pltpu.make_async_remote_copy(
            pbuf.at[h, q], prec.at[h, me if sending else q], p_s.at[h * n + q], recv,
            device_id={"dom": q}, device_id_type=MESH,
        )

    gmrec = (gmrec0, gmrec1)

    def b_copy(h, q, sending):
        recv = b_r.at[h * n + (me if sending else q)]
        return pltpu.make_async_remote_copy(
            msend.at[h, q], gmrec[h].at[me if sending else q], b_s.at[h * n + q], recv,
            device_id={"dom": q}, device_id_type=MESH,
        )

    order = []
    for i in range(half):
        c = lax.rem(me // 2 + 1 + i, half)
        columns = pl.ds(pl.multiple_of(c * 2 * B, 2 * B), 2 * B)
        part = jnp.dot(spread[...], adj[:, columns], preferred_element_type=F32).astype(BF16)
        for h in range(2):
            pbuf[h, 2 * c] = part[h * half_rows : (h + 1) * half_rows, :B]
            pbuf[h, 2 * c + 1] = part[h * half_rows : (h + 1) * half_rows, B:]
        targets = (2 * c, 2 * c + 1) if i < half - 1 else (mate,)
        for q in targets:
            p_copy(0, q, True).start()
            order.append(q)
    for h in range(2):
        prec[h, me] = pbuf[h, me]

    if pieces:
        wgrad_part(across_both, 3)
    else:
        wgrad = lax.dot_general(
            s[...], allg[...], (((1,), (1,)), ((), ())), preferred_element_type=F32
        )
    if scatter:
        if not pieces:
            wpart[...] = wgrad.astype(BF16)

        swap_start(1)
        pair_sum(1)
    else:
        wg[...] = wgrad
        flush_wg = pltpu.make_async_copy(wg, wg_out, lsem.at[10])
        flush_wg.start()

    for q in order:
        p_copy(1, q, True).start()

    for q in dom_peers:
        dom_recv(meta.at[q], mrec.at[q], m_s, m_r, q).wait_recv()
    rc = min(32, half_rows)

    def sum_rows(h, r, _):
        here = pl.ds(pl.multiple_of(r * rc, rc), rc)
        there = pl.ds(pl.multiple_of(h * half_rows + r * rc, rc), rc)
        pick = [mrec[p, 0:1, :].astype(F32) for p in range(n)]
        terms = [prec[h, p, here, :].astype(F32) for p in range(n)]
        back = [jnp.zeros((rc, B), F32) for _ in range(n)]
        for b in range(vb):
            hot = [jnp.where(pick[p] == b, 1.0, 0.0) for p in range(n)]
            total = terms[0] * hot[0]
            for p in range(1, n):
                total = total + terms[p] * hot[p]
            node = total.astype(BF16)
            gn[there, b * B : (b + 1) * B] = node
            node = node.astype(F32)
            back = [back[p] + node * hot[p] for p in range(n)]
        for p in range(n):
            msend[h, p, here, :] = back[p].astype(BF16)
        return 0

    for h in range(2):
        for q in order:
            p_copy(h, q, False).wait_recv()
        lax.fori_loop(0, half_rows // rc, functools.partial(sum_rows, h), 0)
        for q in order:
            b_copy(h, q, True).start()
        gmrec[h][me] = msend[h, me]
        if scatter and h == 0:
            for g in used_groups:
                for q in line_peers:
                    line_copy(g, q, False).wait_recv()
            total = wrec[0].astype(F32)
            for p in range(1, half):
                total = total + wrec[p].astype(F32)
            if pieces:
                for k, source in enumerate((mf, near, far, across_both)):
                    wsum[:, piece_rows(source)] = total[:, k * B : (k + 1) * B].astype(BF16)
            else:
                wsum[...] = total.astype(BF16)
            for q in line_peers:
                dom_send(wsum, span(wg, piece(me), wrows), wg_s, wg_r, q).start()
            wg[pl.ds(pl.multiple_of(piece(me), wrows), wrows), :] = wsum[...]
    flush_gn = pltpu.make_async_copy(gn, gn_out, lsem.at[11])
    flush_gn.start()
    if scatter:
        for q in line_peers:
            dom_recv(wsum, span(wg, piece(q), wrows), wg_s, wg_r, q).wait_recv()
        kept = span(wg, core * half * wrows, half * wrows)
        give = pltpu.make_async_remote_copy(
            kept, kept, x_sem.at[2], x_sem.at[3],
            device_id={"dom": mate}, device_id_type=MESH,
        )
        give.start()

    def place(h, slot, _):
        gm[h * half_rows : (h + 1) * half_rows, pl.ds(pl.multiple_of(slot * B, B), B)] = gmrec[h][
            owner[0, slot]
        ]
        return 0

    flush_gm = []
    for h in range(2):
        for q in order:
            b_copy(h, q, False).wait_recv()
        lax.fori_loop(0, n, functools.partial(place, h), 0, unroll=4)
        part = pl.ds(h * half_rows, half_rows)
        flush_gm.append(pltpu.make_async_copy(gm.at[part], gm_out.at[part], lsem.at[12 + h]))
        flush_gm[h].start()

    if scatter:
        give.wait()
        flush_wg = pltpu.make_async_copy(wg, wg_out, lsem.at[10])
        flush_wg.start()
    for copy in own_sends + passed:
        copy.wait_send()
    for q in dom_peers:
        dom_send(meta.at[q], mrec.at[me], m_s, m_r, q).wait_send()
        for h in range(2):
            p_copy(h, q, True).wait_send()
            b_copy(h, q, True).wait_send()
    if scatter:
        for q in line_peers:
            for g in used_groups:
                line_copy(g, q, True).wait_send()
            dom_send(wsum, span(wg, piece(me), wrows), wg_s, wg_r, q).wait_send()
    flush_gn.wait()
    for copy in flush_gm:
        copy.wait()
    flush_wg.wait()


def finish(gn, gm, wg, gn_out, gm_out, wg_out, gn_v, gm_v, narrow, wide, sem):
    pairs = ((wg, narrow, wide, wg_out), (gm, gm_v, gm_v, gm_out), (gn, gn_v, gn_v, gn_out))
    loads = [pltpu.make_async_copy(p[0], p[1], sem.at[k]) for k, p in enumerate(pairs)]
    stores = [pltpu.make_async_copy(p[2], p[3], sem.at[3 + k]) for k, p in enumerate(pairs)]
    for load in loads:
        load.start()
    loads[0].wait()
    wide[...] = narrow[...].astype(F32)
    stores[0].start()
    for k in (1, 2):
        loads[k].wait()
        stores[k].start()
    for store in stores:
        store.wait()


def body(
    n, m,
    grad_out, saved_agg, weight, tile_values, tile_dst, tile_slot, tile_count,
    mirror_owner, mirror_local,
):
    rows, vertices = grad_out.shape
    features = weight.shape[1]
    vb = vertices // B
    tile_total = tile_values.shape[0]
    scatter = rows % (16 * n) == 0
    wrows = max(rows // n, 16)

    hbm = pl.BlockSpec(memory_space=pltpu.HBM)
    int_rows = functools.partial(pltpu.VMEM, dtype=jnp.int32)
    int_smem = functools.partial(pltpu.SMEM, dtype=jnp.int32)
    pairs = vb * n
    dma = pltpu.SemaphoreType.DMA
    wg_type = BF16 if scatter else F32
    gn, gm, wg = pl.pallas_call(
        functools.partial(kernel, n, m, vb, scatter),
        out_shape=(
            jax.ShapeDtypeStruct((rows, vertices), BF16),
            jax.ShapeDtypeStruct((rows, n * B), BF16),
            jax.ShapeDtypeStruct((rows, features), wg_type),
        ),
        in_specs=[hbm] * 9,
        out_specs=(hbm, hbm, hbm),
        scratch_shapes=[
            int_rows((1, tile_total)),
            int_rows((1, tile_total)),
            int_smem((1, 1)),
            int_smem((1, n)),
            int_smem((1, n)),
            pltpu.VMEM((rows, vertices), BF16),
            pltpu.VMEM((rows, features), BF16),
            pltpu.VMEM((tile_total, B, B), BF16),
            int_rows((1, tile_total)),
            int_rows((1, tile_total)),
            int_rows((1, pairs)),
            int_smem((1, tile_total)),
            int_smem((1, tile_total)),
            int_smem((1, pairs)),
            int_smem((n,)),
            pltpu.VMEM((tile_total + 1, B, B), BF16),
            pltpu.VMEM((vertices, n * B), BF16),
            pltpu.VMEM((features, vertices), BF16),
            pltpu.VMEM((rows, vertices), BF16),
            pltpu.VMEM((n, 16, B), BF16),
            pltpu.VMEM((n, 16, B), BF16),
            pltpu.VMEM((2, n, rows // 2, B), BF16),
            pltpu.VMEM((2, n, rows // 2, B), BF16),
            pltpu.VMEM((2, n, rows // 2, B), BF16),
            pltpu.VMEM((n, rows // 2, B), BF16),
            pltpu.VMEM((n, rows // 2, B), BF16),
            pltpu.VMEM((rows, vertices), BF16),
            pltpu.VMEM((rows, n * B), BF16),
            pltpu.VMEM((rows, features), wg_type),
            pltpu.VMEM((rows, features), BF16),
            pltpu.VMEM((wrows * n // 2, features), BF16),
            pltpu.VMEM((wrows * n // 2, features), BF16),
            pltpu.VMEM((n // 2, wrows, features), BF16),
            pltpu.VMEM((wrows, features), BF16),
            dma((15,)),
            dma((4,)),
            dma((max(m, 6),)), dma((max(m, 6),)),
            dma((n,)), dma((n,)),
            dma((2 * n,)), dma((2 * n,)),
            dma((2 * n,)), dma((2 * n,)),
            dma((2 * n,)), dma((2 * n,)),
            dma((n,)), dma((n,)),
            dma((6,)),
        ],
        compiler_params=pltpu.CompilerParams(
            collective_id=0, has_side_effects=True, vmem_limit_bytes=62 * 1024 * 1024
        ),
        cost_estimate=pl.CostEstimate(
            flops=2 * rows * vertices * (2 * features + n * B),
            bytes_accessed=2 * tile_total * B * B + 8 * rows * vertices,
            transcendentals=0,
        ),
    )(
        tile_dst.reshape(1, -1), tile_slot.reshape(1, -1), tile_count.reshape(1, 1),
        mirror_owner, mirror_local, grad_out, saved_agg, weight, tile_values,
    )
    if scatter:
        return pl.pallas_call(
            finish,
            out_shape=(
                jax.ShapeDtypeStruct(gn.shape, BF16),
                jax.ShapeDtypeStruct(gm.shape, BF16),
                jax.ShapeDtypeStruct(wg.shape, F32),
            ),
            in_specs=[hbm] * 3,
            out_specs=(hbm, hbm, hbm),
            scratch_shapes=[
                pltpu.VMEM(gn.shape, BF16), pltpu.VMEM(gm.shape, BF16),
                pltpu.VMEM(wg.shape, BF16), pltpu.VMEM(wg.shape, F32), dma((6,)),
            ],
        )(gn, gm, wg)
    else:
        wg = lax.psum(wg, "dom")
    return gn, gm, wg


def solution(mesh):
    in_specs = (
        P("feat", "dom"),
        P("feat", "dom"),
        P("feat", None),
        P("dom", None, None),
        P("dom"),
        P("dom"),
        P("dom"),
        P("dom", None),
        P("dom", None),
    )
    out_specs = (P("feat", "dom"), P("feat", "dom"), P("feat", None))
    return jax.shard_map(
        functools.partial(body, mesh.shape["dom"], mesh.shape["feat"]),
        mesh=mesh, in_specs=in_specs, out_specs=out_specs, check_vma=False,
    )
```

```python
import functools

import jax
import jax.numpy as jnp
from jax import lax
from jax.experimental import pallas as pl
from jax.experimental.pallas import tpu as pltpu
from jax.sharding import PartitionSpec as P

MESH = pl.DeviceIdType.MESH
B = 128
F32 = jnp.float32
BF16 = jnp.bfloat16


def kernel(
    n, m, vb, scatter, dst_hbm, slot_hbm, count_hbm, owner_hbm, local_hbm, g, s_hbm, w_hbm, tiles,
    gn_out, gm_out, wg_out,
    dst, slots, count, owner, local, s, w, tbuf, tile_order_v, joins_v, pair_end_v, tile_order,
    joins, pair_end,
    slot_of, run, adj, allg, spread, meta, mrec, pbuf, prec, msend, gmrec0, gmrec1, gn, gm, wg,
    wpart, wmate, wsend, wrec, wsum,
    lsem, tsem, g_s, g_r, m_s, m_r, p_s, p_r, b_s, b_r, ws_s, ws_r, wg_s, wg_r, x_sem,
):
    me = lax.axis_index("dom")
    mf = lax.axis_index("feat")
    rows = g.shape[0]
    tile_total = tiles.shape[0]
    pairs = vb * n
    chunk = tile_total // 4
    dom_peers = [lax.rem(me + k, n) for k in range(1, n)]
    feat_peers = [lax.rem(mf + k, m) for k in range(1, m)]
    core = lax.rem(me, 2)
    mate = me + 1 - 2 * core
    line_peers = [lax.rem(me + 2 * k, n) for k in range(1, n // 2)]

    def load_tiles(i):
        return pltpu.make_async_copy(
            tiles.at[pl.ds(i * chunk, chunk)], tbuf.at[pl.ds(i * chunk, chunk)], tsem.at[i]
        )

    my_rows = pl.ds(pl.multiple_of(mf * rows, rows), rows)
    loads = [
        pltpu.make_async_copy(a, b, lsem.at[i])
        for i, (a, b) in enumerate(
            [(dst_hbm, dst), (slot_hbm, slots), (count_hbm, count), (owner_hbm, owner),
             (local_hbm, local), (w_hbm, w), (s_hbm, s), (g, allg.at[my_rows])]
        )
    ]
    for load in loads:
        load.start()
    for i in range(4):
        load_tiles(i).start()

    barrier = pltpu.get_barrier_semaphore()
    for q in dom_peers:
        pl.semaphore_signal(barrier, inc=1, device_id={"dom": q}, device_id_type=MESH)
    for q in feat_peers:
        pl.semaphore_signal(barrier, inc=1, device_id={"feat": q}, device_id_type=MESH)
    pl.semaphore_wait(barrier, n + m - 2)

    half_rows = rows // 2
    square = m == 4
    near = mf + 1 - 2 * lax.rem(mf, 2)
    far = lax.rem(mf + 2, 4)
    across_both = lax.rem(near + 2, 4)

    def g_copy(source, part, sem, to, whole=False):
        size = rows if whole else half_rows
        start = source * rows + part * half_rows
        there = allg.at[pl.ds(pl.multiple_of(start, half_rows), size)]
        here = there
        if source is mf:
            here = g.at[pl.ds(part * half_rows, size)]
        return pltpu.make_async_remote_copy(
            here, there, g_s.at[sem], g_r.at[sem], device_id={"feat": to}, device_id_type=MESH
        )

    if square:
        own_sends = [
            g_copy(mf, 0, 0, near), g_copy(mf, 1, 2, far),
            g_copy(mf, 1, 1, near), g_copy(mf, 0, 3, far),
        ]
        passed = [g_copy(near, 0, 4, far), g_copy(far, 1, 5, near)]
        first = [g_copy(near, 0, 0, near), g_copy(far, 1, 2, far)]
        second = [g_copy(near, 1, 1, near), g_copy(far, 0, 3, far)]
        last = [g_copy(across_both, 0, 4, far), g_copy(across_both, 1, 5, near)]
    else:
        own_sends = [g_copy(mf, 0, k, q, True) for k, q in enumerate(feat_peers)]
        passed, first, second = [], [], []
        last = [
            g_copy(lax.rem(mf + m - 1 - k, m), 0, k, mf, True) for k in range(m - 1)
        ]

    def dom_send(src, dst, send, recv, q):
        return pltpu.make_async_remote_copy(
            src, dst, send.at[q], recv.at[me], device_id={"dom": q}, device_id_type=MESH
        )

    def dom_recv(src, dst, send, recv, q):
        return pltpu.make_async_remote_copy(
            src, dst, send.at[q], recv.at[q], device_id={"dom": q}, device_id_type=MESH
        )

    for copy in own_sends:
        copy.start()
    for load in loads[:5]:
        load.wait()

    across = lax.broadcasted_iota(jnp.int32, (tile_total, tile_total), 1)
    down = lax.broadcasted_iota(jnp.int32, (tile_total, tile_total), 0)
    key = jnp.broadcast_to(dst[...] * n + slots[...], (tile_total, tile_total))
    key_row = jnp.where(across < count[0, 0], key, pairs)
    key_column = jnp.sum(jnp.where(across == down, key_row, 0), axis=1, keepdims=True)
    earlier = (key_row == key_column) & (across < down)
    rank = jnp.sum(
        jnp.where((key_row < key_column) | earlier, 1, 0), axis=1, keepdims=True
    )
    joined = jnp.max(jnp.where(earlier, 1, 0), axis=1, keepdims=True)
    here = rank == across
    tile_order_v[...] = jnp.sum(jnp.where(here, down, 0), axis=0, keepdims=True)
    joins_v[...] = jnp.sum(jnp.where(here, joined, 0), axis=0, keepdims=True)
    pair = lax.broadcasted_iota(jnp.int32, (tile_total, pairs), 1)
    upto = jnp.sum(jnp.where(key_column <= pair, 1, 0), axis=0, keepdims=True)
    found = jnp.max(jnp.where(key_column == pair, 1, 0), axis=0, keepdims=True)
    pair_end_v[...] = upto * found
    link_copies = [
        pltpu.make_async_copy(tile_order_v, tile_order, lsem.at[8]),
        pltpu.make_async_copy(joins_v, joins, lsem.at[14]),
        pltpu.make_async_copy(pair_end_v, pair_end, lsem.at[9]),
    ]
    for copy in link_copies:
        copy.start()

    def fill_meta(o, _):
        slot = lax.fori_loop(
            0, n, lambda k, acc: jnp.where(owner[0, k] == o, k, acc), jnp.int32(0), unroll=8
        )
        slot_of[o] = slot
        value = local[0, slot].astype(F32)
        meta[o] = jnp.full((16, B), value, F32).astype(BF16)
        return 0

    lax.fori_loop(0, n, fill_meta, 0)
    for q in dom_peers:
        dom_send(meta.at[q], mrec.at[me], m_s, m_r, q).start()
    mrec[me] = meta[me]

    for copy in link_copies:
        copy.wait()
    run[0] = jnp.zeros((B, B), BF16)
    for i in range(4):
        load_tiles(i).wait()

    def add_tile(t, acc):
        acc = acc * joins[0, t].astype(F32) + tbuf[tile_order[0, t]].astype(F32)
        run[t + 1] = acc.astype(BF16)
        return acc

    acc = jnp.zeros((B, B), F32)
    for i in range(4):
        acc = lax.fori_loop(i * chunk, (i + 1) * chunk, add_tile, acc, unroll=4)
        if i == 1:
            for arrived, on in zip(first, passed):
                arrived.wait_recv()
                on.start()

    def fill_owner(o, _):
        slot = slot_of[o]
        for d in range(vb):
            adj[d * B : (d + 1) * B, pl.ds(pl.multiple_of(o * B, B), B)] = run[
                pair_end[0, d * n + slot]
            ]
        return 0

    lax.fori_loop(0, n, fill_owner, 0)

    for load in loads[5:]:
        load.wait()

    def piece_rows(source):
        return pl.ds(pl.multiple_of(source * rows, rows), rows)

    def back_part(source):
        here = piece_rows(source)
        return jnp.dot(w[:, here], allg[here, :], preferred_element_type=F32)

    def wgrad_part(source, k):
        here = piece_rows(source)
        value = lax.dot_general(
            s[...], allg[here, :], (((1,), (1,)), ((), ())), preferred_element_type=F32
        )
        wpart[:, k * B : (k + 1) * B] = value.astype(BF16)

    pieces = square and scatter and rows % B == 0
    half = n // 2
    wrows = rows // n
    features = w.shape[1]
    groups = ((0, features - B), (features - B, B)) if pieces else ((0, 0), (0, features))

    def span(ref, start, size, g=None):
        here = pl.ds(pl.multiple_of(start, wrows), size)
        return ref.at[here] if g is None else ref.at[here, pl.ds(*groups[g])]

    def piece(q):
        return (lax.rem(q, 2) * half + q // 2) * wrows

    def swap_copy(g):
        return pltpu.make_async_remote_copy(
            span(wpart, (1 - core) * half * wrows, half * wrows, g),
            wmate.at[:, pl.ds(*groups[g])],
            x_sem.at[4 * g], x_sem.at[4 * g + 1], device_id={"dom": mate}, device_id_type=MESH,
        )

    def line_copy(g, q, sending):
        there = me // 2 if sending else q // 2
        return pltpu.make_async_remote_copy(
            span(wsend, q // 2 * wrows, wrows, g), wrec.at[there, :, pl.ds(*groups[g])],
            ws_s.at[g * n + q], ws_r.at[g * n + (me if sending else q)],
            device_id={"dom": q}, device_id_type=MESH,
        )

    def swap_start(g):
        swap_copy(g).start()

    def pair_sum(g):
        swap_copy(g).wait()
        lanes = pl.ds(*groups[g])
        mine = wpart[pl.ds(pl.multiple_of(core * half * wrows, wrows), half * wrows), lanes]
        wsend[:, lanes] = (mine.astype(F32) + wmate[:, lanes].astype(F32)).astype(BF16)
        for q in line_peers:
            line_copy(g, q, True).start()
        own = wsend[pl.ds(pl.multiple_of(me // 2 * wrows, wrows), wrows), lanes]
        wrec[me // 2, :, lanes] = own

    used_groups = (0, 1) if pieces else (1,)
    if pieces:
        back = back_part(mf)
        wgrad_part(mf, 0)
        for copy in second:
            copy.wait_recv()
        back = back + back_part(near) + back_part(far)
        wgrad_part(near, 1)
        wgrad_part(far, 2)
        swap_start(0)
        pair_sum(0)
        for copy in last:
            copy.wait_recv()
        spread[...] = (back + back_part(across_both)).astype(BF16)
    else:
        for copy in second + last:
            copy.wait_recv()
        spread[...] = jnp.dot(w[...], allg[...], preferred_element_type=F32).astype(BF16)

    def p_copy(h, q, sending):
        recv = p_r.at[h * n + (me if sending else q)]
        return pltpu.make_async_remote_copy(
            pbuf.at[h, q], prec.at[h, me if sending else q], p_s.at[h * n + q], recv,
            device_id={"dom": q}, device_id_type=MESH,
        )

    gmrec = (gmrec0, gmrec1)

    def b_copy(h, q, sending):
        recv = b_r.at[h * n + (me if sending else q)]
        return pltpu.make_async_remote_copy(
            msend.at[h, q], gmrec[h].at[me if sending else q], b_s.at[h * n + q], recv,
            device_id={"dom": q}, device_id_type=MESH,
        )

    order = []
    for i in range(half):
        c = lax.rem(me // 2 + 1 + i, half)
        columns = pl.ds(pl.multiple_of(c * 2 * B, 2 * B), 2 * B)
        part = jnp.dot(spread[...], adj[:, columns], preferred_element_type=F32).astype(BF16)
        for h in range(2):
            pbuf[h, 2 * c] = part[h * half_rows : (h + 1) * half_rows, :B]
            pbuf[h, 2 * c + 1] = part[h * half_rows : (h + 1) * half_rows, B:]
        targets = (2 * c, 2 * c + 1) if i < half - 1 else (mate,)
        for q in targets:
            p_copy(0, q, True).start()
            order.append(q)
    for h in range(2):
        prec[h, me] = pbuf[h, me]

    if pieces:
        wgrad_part(across_both, 3)
    else:
        wgrad = lax.dot_general(
            s[...], allg[...], (((1,), (1,)), ((), ())), preferred_element_type=F32
        )
    if scatter:
        if not pieces:
            wpart[...] = wgrad.astype(BF16)

        swap_start(1)
        pair_sum(1)
    else:
        wg[...] = wgrad
        flush_wg = pltpu.make_async_copy(wg, wg_out, lsem.at[10])
        flush_wg.start()

    for q in order:
        p_copy(1, q, True).start()

    for q in dom_peers:
        dom_recv(meta.at[q], mrec.at[q], m_s, m_r, q).wait_recv()
    rc = min(16, half_rows)

    def sum_rows(h, r, _):
        here = pl.ds(pl.multiple_of(r * rc, rc), rc)
        there = pl.ds(pl.multiple_of(h * half_rows + r * rc, rc), rc)
        pick = [mrec[p, 0:1, :].astype(F32) for p in range(n)]
        terms = [prec[h, p, here, :].astype(F32) for p in range(n)]
        back = [jnp.zeros((rc, B), F32) for _ in range(n)]
        for b in range(vb):
            hot = [jnp.where(pick[p] == b, 1.0, 0.0) for p in range(n)]
            total = terms[0] * hot[0]
            for p in range(1, n):
                total = total + terms[p] * hot[p]
            node = total.astype(BF16)
            gn[there, b * B : (b + 1) * B] = node
            node = node.astype(F32)
            back = [back[p] + node * hot[p] for p in range(n)]
        for p in range(n):
            msend[h, p, here, :] = back[p].astype(BF16)
        return 0

    for h in range(2):
        for q in order:
            p_copy(h, q, False).wait_recv()
        lax.fori_loop(0, half_rows // rc, functools.partial(sum_rows, h), 0)
        for q in order:
            b_copy(h, q, True).start()
        gmrec[h][me] = msend[h, me]
        if scatter and h == 0:
            for g in used_groups:
                for q in line_peers:
                    line_copy(g, q, False).wait_recv()
            total = wrec[0].astype(F32)
            for p in range(1, half):
                total = total + wrec[p].astype(F32)
            if pieces:
                for k, source in enumerate((mf, near, far, across_both)):
                    wsum[:, piece_rows(source)] = total[:, k * B : (k + 1) * B].astype(BF16)
            else:
                wsum[...] = total.astype(BF16)
            for q in line_peers:
                dom_send(wsum, span(wg, piece(me), wrows), wg_s, wg_r, q).start()
            wg[pl.ds(pl.multiple_of(piece(me), wrows), wrows), :] = wsum[...]
    flush_gn = pltpu.make_async_copy(gn, gn_out, lsem.at[11])
    flush_gn.start()
    if scatter:
        for q in line_peers:
            dom_recv(wsum, span(wg, piece(q), wrows), wg_s, wg_r, q).wait_recv()
        kept = span(wg, core * half * wrows, half * wrows)
        give = pltpu.make_async_remote_copy(
            kept, kept, x_sem.at[2], x_sem.at[3],
            device_id={"dom": mate}, device_id_type=MESH,
        )
        give.start()

    def place(h, slot, _):
        gm[h * half_rows : (h + 1) * half_rows, pl.ds(pl.multiple_of(slot * B, B), B)] = gmrec[h][
            owner[0, slot]
        ]
        return 0

    flush_gm = []
    for h in range(2):
        for q in order:
            b_copy(h, q, False).wait_recv()
        lax.fori_loop(0, n, functools.partial(place, h), 0, unroll=4)
        part = pl.ds(h * half_rows, half_rows)
        flush_gm.append(pltpu.make_async_copy(gm.at[part], gm_out.at[part], lsem.at[12 + h]))
        flush_gm[h].start()

    if scatter:
        give.wait()
        flush_wg = pltpu.make_async_copy(wg, wg_out, lsem.at[10])
        flush_wg.start()
    for copy in own_sends + passed:
        copy.wait_send()
    for q in dom_peers:
        dom_send(meta.at[q], mrec.at[me], m_s, m_r, q).wait_send()
        for h in range(2):
            p_copy(h, q, True).wait_send()
            b_copy(h, q, True).wait_send()
    if scatter:
        for q in line_peers:
            for g in used_groups:
                line_copy(g, q, True).wait_send()
            dom_send(wsum, span(wg, piece(me), wrows), wg_s, wg_r, q).wait_send()
    flush_gn.wait()
    for copy in flush_gm:
        copy.wait()
    flush_wg.wait()


def finish(gn, gm, wg, gn_out, gm_out, wg_out, gn_v, gm_v, narrow, wide, sem):
    pairs = ((wg, narrow, wide, wg_out), (gm, gm_v, gm_v, gm_out), (gn, gn_v, gn_v, gn_out))
    loads = [pltpu.make_async_copy(p[0], p[1], sem.at[k]) for k, p in enumerate(pairs)]
    stores = [pltpu.make_async_copy(p[2], p[3], sem.at[3 + k]) for k, p in enumerate(pairs)]
    for load in loads:
        load.start()
    loads[0].wait()
    wide[...] = narrow[...].astype(F32)
    stores[0].start()
    for k in (1, 2):
        loads[k].wait()
        stores[k].start()
    for store in stores:
        store.wait()


def body(
    n, m,
    grad_out, saved_agg, weight, tile_values, tile_dst, tile_slot, tile_count,
    mirror_owner, mirror_local,
):
    rows, vertices = grad_out.shape
    features = weight.shape[1]
    vb = vertices // B
    tile_total = tile_values.shape[0]
    scatter = rows % (16 * n) == 0
    wrows = max(rows // n, 16)

    hbm = pl.BlockSpec(memory_space=pltpu.HBM)
    int_rows = functools.partial(pltpu.VMEM, dtype=jnp.int32)
    int_smem = functools.partial(pltpu.SMEM, dtype=jnp.int32)
    pairs = vb * n
    dma = pltpu.SemaphoreType.DMA
    wg_type = BF16 if scatter else F32
    gn, gm, wg = pl.pallas_call(
        functools.partial(kernel, n, m, vb, scatter),
        out_shape=(
            jax.ShapeDtypeStruct((rows, vertices), BF16),
            jax.ShapeDtypeStruct((rows, n * B), BF16),
            jax.ShapeDtypeStruct((rows, features), wg_type),
        ),
        in_specs=[hbm] * 9,
        out_specs=(hbm, hbm, hbm),
        scratch_shapes=[
            int_rows((1, tile_total)),
            int_rows((1, tile_total)),
            int_smem((1, 1)),
            int_smem((1, n)),
            int_smem((1, n)),
            pltpu.VMEM((rows, vertices), BF16),
            pltpu.VMEM((rows, features), BF16),
            pltpu.VMEM((tile_total, B, B), BF16),
            int_rows((1, tile_total)),
            int_rows((1, tile_total)),
            int_rows((1, pairs)),
            int_smem((1, tile_total)),
            int_smem((1, tile_total)),
            int_smem((1, pairs)),
            int_smem((n,)),
            pltpu.VMEM((tile_total + 1, B, B), BF16),
            pltpu.VMEM((vertices, n * B), BF16),
            pltpu.VMEM((features, vertices), BF16),
            pltpu.VMEM((rows, vertices), BF16),
            pltpu.VMEM((n, 16, B), BF16),
            pltpu.VMEM((n, 16, B), BF16),
            pltpu.VMEM((2, n, rows // 2, B), BF16),
            pltpu.VMEM((2, n, rows // 2, B), BF16),
            pltpu.VMEM((2, n, rows // 2, B), BF16),
            pltpu.VMEM((n, rows // 2, B), BF16),
            pltpu.VMEM((n, rows // 2, B), BF16),
            pltpu.VMEM((rows, vertices), BF16),
            pltpu.VMEM((rows, n * B), BF16),
            pltpu.VMEM((rows, features), wg_type),
            pltpu.VMEM((rows, features), BF16),
            pltpu.VMEM((wrows * n // 2, features), BF16),
            pltpu.VMEM((wrows * n // 2, features), BF16),
            pltpu.VMEM((n // 2, wrows, features), BF16),
            pltpu.VMEM((wrows, features), BF16),
            dma((15,)),
            dma((4,)),
            dma((max(m, 6),)), dma((max(m, 6),)),
            dma((n,)), dma((n,)),
            dma((2 * n,)), dma((2 * n,)),
            dma((2 * n,)), dma((2 * n,)),
            dma((2 * n,)), dma((2 * n,)),
            dma((n,)), dma((n,)),
            dma((6,)),
        ],
        compiler_params=pltpu.CompilerParams(
            collective_id=0, has_side_effects=True, vmem_limit_bytes=62 * 1024 * 1024
        ),
        cost_estimate=pl.CostEstimate(
            flops=2 * rows * vertices * (2 * features + n * B),
            bytes_accessed=2 * tile_total * B * B + 8 * rows * vertices,
            transcendentals=0,
        ),
    )(
        tile_dst.reshape(1, -1), tile_slot.reshape(1, -1), tile_count.reshape(1, 1),
        mirror_owner, mirror_local, grad_out, saved_agg, weight, tile_values,
    )
    if scatter:
        return pl.pallas_call(
            finish,
            out_shape=(
                jax.ShapeDtypeStruct(gn.shape, BF16),
                jax.ShapeDtypeStruct(gm.shape, BF16),
                jax.ShapeDtypeStruct(wg.shape, F32),
            ),
            in_specs=[hbm] * 3,
            out_specs=(hbm, hbm, hbm),
            scratch_shapes=[
                pltpu.VMEM(gn.shape, BF16), pltpu.VMEM(gm.shape, BF16),
                pltpu.VMEM(wg.shape, BF16), pltpu.VMEM(wg.shape, F32), dma((6,)),
            ],
        )(gn, gm, wg)
    else:
        wg = lax.psum(wg, "dom")
    return gn, gm, wg


def solution(mesh):
    in_specs = (
        P("feat", "dom"),
        P("feat", "dom"),
        P("feat", None),
        P("dom", None, None),
        P("dom"),
        P("dom"),
        P("dom"),
        P("dom", None),
        P("dom", None),
    )
    out_specs = (P("feat", "dom"), P("feat", "dom"), P("feat", None))
    return jax.shard_map(
        functools.partial(body, mesh.shape["dom"], mesh.shape["feat"]),
        mesh=mesh, in_specs=in_specs, out_specs=out_specs, check_vma=False,
    )
```
